256 devices in a mesh: ctx: 32 (over z, x_lo, core), head: 8 (over x_hi, y).
Axes of the slice: x: 4 (x_hi: 2, x_lo: 2; x = x_hi * 2 + x_lo), y: 4, z: 8, core: 2. Of those that a mesh axis runs over, the one named last changes fastest.
Arguments:
- queries: bfloat16 [8192, 6144], P(('ctx', 'head')), may hold values from -113 to 113
- keys: bfloat16 [8192, 1024], P(('ctx', 'head')), may hold values from -4.6 to 4.6
- values: bfloat16 [8192, 1024], P(('ctx', 'head')), may hold values from -6 to 6
- fold_map: int32 [64], replicated, may hold values from 0 to 63, each once
- noisy: int32 [64], replicated, may hold values from 0 to 1, as said below
- noise_step: int32 [64], replicated, may hold values from 0 to 63
- gate_table: float32 [64, 6144], P(None, 'head'), may hold values from -1.5 to 1.5
Outputs:
- gated_update: bfloat16 [8192, 6144], P(('ctx', 'head'))
The draws below stay inside these ranges and needn't reach their ends.
Inputs may be any that keep to these rules, and one draw needn't show every extreme that they name: `fold_map`: each position in span order appears once. The noisy spans are a trailing run of the span order holding between 16 and 48 spans.
All inputs are finite; a program needn't handle non-finite values.
Results may differ from the reference program's by a relative error of at most 0.006.
Values may be sent and summed in bfloat16 or wider, within the bound.
A program may use at most 64 MiB of HBM per device.

```python
import jax
import jax.numpy as jnp
from jax import lax

HEADS = 48
KVH = 8
HD = 128
D = 6144
SPAN = 128
STEPS = 64
NCH = 64
TOKENS = 8192


def shared_keys(key):
    return jnp.clip(jax.random.normal(key, (TOKENS, KVH * HD), jnp.float32), -4.5, 4.5)


def draw_keys(key, part):
    base = shared_keys(key)
    return base.astype(jnp.bfloat16)


def draw_queries(key, part):
    key = jax.random.fold_in(key, 5)
    return (2.5 * jnp.clip(jax.random.normal(key, (TOKENS, HEADS * HD), jnp.float32), -6.0, 6.0)).astype(jnp.bfloat16)


def draw_noisy(key, part):
    key = jax.random.fold_in(key, 11)
    cutoff = jax.random.randint(key, (), NCH // 4, 3 * NCH // 4 + 1)
    return (jnp.arange(NCH, dtype=jnp.int32) >= cutoff).astype(jnp.int32)


def place_ends(entries, rng, least, high):
    shape = entries.shape
    spot = [jax.random.randint(jax.random.fold_in(rng, axis), (), 0, shape[axis]) for axis in range(len(shape))]
    entries = entries.at[tuple(spot)].set(least)
    longest = shape.index(max(shape))
    spot[longest] = (spot[longest] + 1) % shape[longest]
    return entries.at[tuple(spot)].set(high)


def block_scale(rng, extent, cuts, least, top_value):
    def one(position, blocks):
        steps = jax.random.uniform(jax.random.fold_in(jax.random.fold_in(rng, 6), position), (blocks,), jnp.float32, least / len(cuts), top_value / len(cuts))
        return jnp.repeat(jnp.exp(steps), extent[position] // blocks).reshape((-1,) + (1,) * (len(extent) - position - 1))

    gain = one(*cuts[0])
    for cut in cuts[1:]:
        gain = gain * one(*cut)
    return gain


def gaussian(stream_key, shape, deviation, most, cuts=(), kind=jnp.bfloat16):
    array = jax.random.normal(stream_key, shape, jnp.float32) * deviation
    if len(cuts) > 0:
        array = block_scale(stream_key, shape, cuts, -0.22, 0.18) * array
    return jnp.clip(array, min=-most, max=most).astype(kind)


def setup_inputs(seed: int = 0) -> dict:
    key_list = jax.random.split(jax.random.key(seed), 8)
    queries = draw_queries(jax.random.fold_in(key_list[7], 71), 0)
    keys = draw_keys(jax.random.fold_in(key_list[7], 71), 0)
    values = gaussian(key_list[2], (TOKENS, KVH * HD), 1.0, 6.0, ((0, 256),))
    fold_map = jax.random.permutation(key_list[3], NCH).astype(jnp.int32)
    noisy = draw_noisy(jax.random.fold_in(key_list[7], 71), 0)
    noise_step = place_ends(jax.random.randint(key_list[5], (NCH,), 0, STEPS), jax.random.fold_in(key_list[5], 1), 0, STEPS - 1).astype(jnp.int32)
    gate_table = jnp.clip(jax.random.uniform(key_list[6], (STEPS, D), jnp.float32, -1.5, 1.5) * block_scale(key_list[6], (STEPS, D), ((1, 8),), -0.4, 0.0), -1.5, 1.5)
    return dict(queries=queries, keys=keys, values=values, fold_map=fold_map, noisy=noisy, noise_step=noise_step, gate_table=gate_table)


def reference(queries, keys, values, fold_map, noisy, noise_step, gate_table):
    ratio = HEADS // KVH
    scale = HD ** -0.5
    token_order = jnp.repeat(fold_map, SPAN)
    seen = token_order[None, :] <= token_order[:, None]
    head_queries = jnp.transpose(queries.reshape(TOKENS, HEADS, HD), (1, 0, 2))
    group_keys = jnp.transpose(keys.reshape(TOKENS, KVH, HD), (1, 0, 2))
    group_values = jnp.transpose(values.reshape(TOKENS, KVH, HD), (1, 0, 2))

    def one_head(head_number):
        group = head_number // ratio
        query_rows = head_queries[head_number]
        key_rows = group_keys[group]
        value_rows = group_values[group]
        scores = jnp.dot(query_rows, key_rows.T, preferred_element_type=jnp.float32) * scale
        scores = jnp.where(seen, scores, -jnp.inf)
        highest = jnp.max(scores, axis=1, keepdims=True)
        probs = jnp.exp(scores - highest)
        totals = jnp.sum(probs, axis=1, keepdims=True)
        summed = jnp.dot(probs.astype(jnp.bfloat16), value_rows, preferred_element_type=jnp.float32)
        return summed / totals

    attended = lax.map(one_head, jnp.arange(HEADS, dtype=jnp.int32))
    attended = jnp.transpose(attended, (1, 0, 2)).reshape(TOKENS, HEADS * HD)
    gate = gate_table[noise_step[token_order]]
    live = noisy[token_order] == 1
    return jnp.where(live[:, None], gate * attended, jnp.float32(0.0)).astype(jnp.bfloat16)
```

```python
import functools
import math

import jax
import jax.numpy as jnp
from jax import lax
from jax.experimental import pallas as pl
from jax.experimental.pallas import tpu as pltpu
from jax.sharding import PartitionSpec as P

HEADS = 48
KVH = 8
HD = 128
SPAN = 128
NZ = 8
NH = 8
RATIO = HEADS // KVH
ROWS = 32
BLOCK = NH * ROWS
GROUP = 4 * BLOCK
FEAT = RATIO * HD
TILE = 256
TILES = 2 * SPAN * RATIO // TILE
VROWS = HD + 16
NEG = -1e30
MESH = pl.DeviceIdType.MESH
K, V = 0, 1


def kernel(
    q_ref, k_ref, v_ref, fold, noisy, noise_step, gate_ref, out_ref,
    q_in, k_buf, v_in, vt_buf, qt, m_s, acc, gate_v, ost,
    a2a_send, a2a_recv, loc_sem, kv_send, kv_recv, out_send, out_recv,
):
    me = lax.axis_index("ctx")
    h = lax.axis_index("head")
    z = lax.div(me, 4)
    x = lax.rem(lax.div(me, 2), 2)
    c = lax.rem(me, 2)
    xh = lax.div(h, 4)
    y = lax.rem(h, 4)

    def ctx_of(dz, x_, c_):
        return lax.rem(z + (dz + NZ), NZ) * 4 + x_ * 2 + c_

    zp, zm = ctx_of(1, x, c), ctx_of(-1, x, c)
    xb, sib = ctx_of(0, 1 - x, c), ctx_of(0, x, 1 - c)
    peers = [lax.rem(h + r, NH) for r in range(1, NH)]

    own_k = pltpu.make_async_copy(
        k_ref.at[:, pl.ds(pl.multiple_of(h * HD, HD), HD)],
        k_buf.at[me, pl.ds(pl.multiple_of(h * ROWS, ROWS), ROWS), :], loc_sem.at[0])
    own_v = pltpu.make_async_copy(
        v_ref.at[:, pl.ds(pl.multiple_of(h * HD, HD), HD)],
        v_in.at[pl.ds(pl.multiple_of(h * ROWS, ROWS), ROWS), :], loc_sem.at[1])
    own_q = pltpu.make_async_copy(
        q_ref.at[:, pl.ds(pl.multiple_of(h * FEAT, FEAT), FEAT)], q_in.at[h], loc_sem.at[2])
    gates = pltpu.make_async_copy(gate_ref, gate_v, loc_sem.at[3])
    own_k.start()
    own_v.start()
    own_q.start()
    gates.start()

    barrier = pltpu.get_barrier_semaphore()
    for peer in peers:
        pl.semaphore_signal(barrier, inc=1, device_id=(me, peer), device_id_type=MESH)
    for other in (zp, zm, xb, sib):
        pl.semaphore_signal(barrier, inc=1, device_id=(other, h), device_id_type=MESH)
    vt_buf[:, HD:, :] = jnp.ones((NZ * 4, VROWS - HD, BLOCK), jnp.bfloat16)
    m_s[...] = jnp.full_like(m_s, NEG)
    acc[...] = jnp.zeros_like(acc)
    pl.semaphore_wait(barrier, NH - 1 + 4)

    def k_copy(i, peer, source):
        return pltpu.make_async_remote_copy(
            k_ref.at[:, pl.ds(pl.multiple_of(peer * HD, HD), HD)],
            k_buf.at[me, pl.ds(pl.multiple_of(source * ROWS, ROWS), ROWS), :],
            a2a_send.at[0, i], a2a_recv.at[0, source], device_id=(me, peer), device_id_type=MESH)

    def v_copy(i, peer, source):
        return pltpu.make_async_remote_copy(
            v_ref.at[:, pl.ds(pl.multiple_of(peer * HD, HD), HD)],
            v_in.at[pl.ds(pl.multiple_of(source * ROWS, ROWS), ROWS), :],
            a2a_send.at[1, i], a2a_recv.at[1, source], device_id=(me, peer), device_id_type=MESH)

    def q_copy(i, peer, source):
        return pltpu.make_async_remote_copy(
            q_ref.at[:, pl.ds(pl.multiple_of(peer * FEAT, FEAT), FEAT)], q_in.at[source],
            a2a_send.at[2, i], a2a_recv.at[2, source], device_id=(me, peer), device_id_type=MESH)

    for i, peer in enumerate(peers):
        k_copy(i, peer, h).start()
    for i, peer in enumerate(peers):
        v_copy(i, peer, h).start()
    for i, peer in enumerate(peers):
        q_copy(i, peer, h).start()

    sent = []

    def block_copy(half, block, target, send):
        ref = k_buf.at[block] if half == K else vt_buf.at[block, pl.ds(0, HD), :]
        return pltpu.make_async_remote_copy(
            ref, ref, kv_send.at[send], kv_recv.at[half, block],
            device_id=(target, h), device_id_type=MESH)

    def send(half, block, *targets):
        for target in targets:
            block_copy(half, block, target, len(sent)).start()
            sent.append((half, block, target))

    def arrived(half, block):
        block_copy(half, block, sib, 0).wait_recv()

    own = lambda d: ctx_of(d, x, c)
    oth = lambda d: ctx_of(d, 1 - x, c)

    own_k.wait()
    for i, peer in enumerate(peers):
        k_copy(i, peer, peer).wait_recv()
    send(K, me, xb, zp, zm, sib)
    own_v.wait()
    for i, peer in enumerate(peers):
        v_copy(i, peer, peer).wait_recv()
    vt_buf[me, :HD, :] = v_in[...].astype(jnp.float32).T.astype(jnp.bfloat16)
    send(V, me, xb, zp, zm, sib)

    arrived(K, oth(0))
    send(K, oth(0), zp, zm, sib)
    arrived(V, oth(0))
    send(V, oth(0), sib)

    def own_came(d):
        for sign, onward in ((-1, zp), (1, zm)):
            block = own(sign * d)
            arrived(K, block)
            send(K, block, *((onward,) if d < 3 or sign < 0 else ()), sib)
        for sign, onward in ((-1, zp), (1, zm)):
            block = own(sign * d)
            arrived(V, block)
            send(V, block, *((onward,) if d < 3 or sign > 0 else ()), xb, sib)

    def oth_came(d):
        for sign, onward in ((-1, zp), (1, zm)):
            block = oth(sign * d)
            arrived(K, block)
            send(K, block, *((onward,) if d < 3 else ()), sib)
        for sign in (-1, 1):
            block = oth(sign * d)
            arrived(V, block)
            send(V, block, sib)

    def own_last():
        arrived(K, own(4))
        send(K, own(4), xb, sib)
        arrived(V, own(4))
        send(V, own(4), xb, sib)

    def oth_last():
        arrived(K, oth(4))
        send(K, oth(4), sib)
        arrived(V, oth(4))
        send(V, oth(4), sib)

    def sibling(d):
        for x_ in (0, 1):
            for half in (K, V):
                arrived(half, ctx_of(d, x_, 1 - c))

    own_came(1)

    own_q.wait()
    for i, peer in enumerate(peers):
        q_copy(i, peer, peer).wait_recv()
    factor = math.log2(math.e) / math.sqrt(HD)
    spans = [1 - xh, xh]
    for slot in range(2):
        for j in range(RATIO):
            part = q_in[pl.ds(spans[slot] * 4, 4), :, j * HD:(j + 1) * HD].reshape(SPAN, HD)
            scaled = (part.astype(jnp.float32) * factor).T
            high = scaled.astype(jnp.bfloat16)
            low = (scaled - high.astype(jnp.float32)).astype(jnp.bfloat16)
            at = (slot * RATIO + j) * HD
            qt[0:HD, at:at + HD] = high
            qt[HD:2 * HD, at:at + HD] = low

    my_order = [fold[2 * me + s] for s in spans]
    gate_rows = [gate_v.at[pl.ds(noise_step[o], 1), :] for o in my_order]
    live = [noisy[o] == 1 for o in my_order]

    def work(zq, done=None):
        keys = k_buf[pl.ds(zq * 4, 4)].reshape(GROUP, HD)
        keys = jnp.concatenate([keys, keys], axis=1)
        values = jnp.concatenate([vt_buf[zq * 4 + i] for i in range(4)], axis=1)
        count = GROUP // SPAN
        orders = [fold[zq * count + i] for i in range(count)]
        hide = [
            [jnp.where(o <= mine, jnp.float32(0), jnp.float32(NEG)) for o in orders]
            for mine in my_order
        ]

        def score(t):
            return jnp.dot(keys, qt[:, t * TILE:(t + 1) * TILE], preferred_element_type=jnp.float32)

        def soften(t, s):
            cols = slice(t * TILE, (t + 1) * TILE)
            bias = hide[t // (TILES // 2)]
            before = m_s[0:1, cols]
            top = before
            for i in range(count):
                top = jnp.maximum(top, jnp.max(s[i * SPAN:(i + 1) * SPAN], axis=0, keepdims=True) + bias[i])
            probs = [
                jnp.exp2(s[i * SPAN:(i + 1) * SPAN] - (top - 2 * bias[i])).astype(jnp.bfloat16)
                for i in range(count)
            ]
            m_s[0:1, cols] = top
            return jnp.concatenate(probs, axis=0), jnp.exp2(before - top)

        def add(t, probs, alpha):
            cols = slice(t * TILE, (t + 1) * TILE)
            total = acc[:, cols] * alpha + jnp.dot(values, probs, preferred_element_type=jnp.float32)
            if done is None:
                acc[:, cols] = total
            else:
                done(t, total)

        s = score(0)
        held = None
        for t in range(TILES):
            following = score(t + 1) if t + 1 < TILES else None
            if held is not None:
                add(t - 1, *held)
            held = soften(t, s)
            s = following
        add(TILES - 1, *held)

    events = {
        0: [lambda: oth_came(1)],
        1: [lambda: own_came(2)],
        2: [lambda: oth_came(2)],
        3: [lambda: own_came(3)],
        4: [lambda: oth_came(3), own_last],
        6: [oth_last],
    }

    sibling(0)

    def step(i, carry):
        for at, todo in events.items():
            if at < NZ - 1:
                @pl.when(i == at)
                def _():
                    for f in todo:
                        f()
        for d in (1, 2, 3):
            @pl.when(i == 2 * d - 1)
            def _():
                sibling(d)
                sibling(-d)
        near = lax.div(i + 1, 2)
        d = jnp.where(lax.rem(i, 2) == 1, near, NZ - near)
        work(lax.rem(z + d, NZ))
        return carry

    lax.fori_loop(0, NZ - 1, step, 0)
    sibling(4)

    results = []

    def result_copy(t, target, part, i):
        jp = t % 3
        src = ost.at[t, pl.ds(pl.multiple_of(part * ROWS, ROWS), ROWS), :]
        dst = out_ref.at[:, pl.ds(pl.multiple_of(h * FEAT + jp * TILE, TILE), TILE)]
        return pltpu.make_async_remote_copy(
            src, dst, out_send.at[i], out_recv.at[h, jp],
            device_id=(me, target), device_id_type=MESH)

    def own_result(t):
        jp = t % 3
        return pltpu.make_async_copy(
            ost.at[t, pl.ds(pl.multiple_of(y * ROWS, ROWS), ROWS), :],
            out_ref.at[:, pl.ds(pl.multiple_of(h * FEAT + jp * TILE, TILE), TILE)],
            loc_sem.at[4 + jp])

    gates.wait()

    def done(t, total):
        slot = t // 3
        jp = t % 3
        scaled = total[:HD] * (1.0 / total[HD:HD + 1])
        for jj in range(2):
            j = 2 * jp + jj
            rows = scaled[:, jj * HD:(jj + 1) * HD].T
            rows = rows * gate_rows[slot][:, j * HD:(j + 1) * HD]
            rows = jnp.where(live[slot], rows, jnp.float32(0))
            ost[t, :, jj * HD:(jj + 1) * HD] = rows.astype(jnp.bfloat16)
        for r in range(4):
            part = lax.rem(y + r, 4)
            if slot == 1 and r == 0:
                own_result(t).start()
                continue
            i = len(results)
            target = spans[slot] * 4 + part
            result_copy(t, target, part, i).start()
            results.append((t, target, part))

    work(lax.rem(z + 4, NZ), done)

    for jp in range(3):
        own_result(3 + jp).wait()
    for i, (t, target, part) in enumerate(results):
        result_copy(t, target, part, i).wait_send()
    for i, peer in enumerate(peers):
        k_copy(i, peer, h).wait_send()
        v_copy(i, peer, h).wait_send()
        q_copy(i, peer, h).wait_send()
    for i, (half, block, target) in enumerate(sent):
        block_copy(half, me, sib, i).wait_send()
    for peer in peers:
        for jp in range(3):
            pltpu.make_async_remote_copy(
                ost.at[0, pl.ds(0, ROWS), :],
                out_ref.at[:, pl.ds(pl.multiple_of(peer * FEAT + jp * TILE, TILE), TILE)],
                out_send.at[0], out_recv.at[peer, jp],
                device_id=(me, peer), device_id_type=MESH).wait_recv()


def local(queries, keys, values, fold_map, noisy, noise_step, gate_table):
    hbm = pl.BlockSpec(memory_space=pl.ANY)
    smem = pl.BlockSpec(memory_space=pltpu.SMEM)
    width = 2 * SPAN * RATIO
    blocks = NZ * 4
    return pl.pallas_call(
        kernel,
        out_shape=jax.ShapeDtypeStruct(queries.shape, queries.dtype),
        in_specs=[hbm, hbm, hbm, smem, smem, smem, hbm],
        out_specs=hbm,
        scratch_shapes=[
            pltpu.VMEM((NH, ROWS, FEAT), jnp.bfloat16),
            pltpu.VMEM((blocks, BLOCK, HD), jnp.bfloat16),
            pltpu.VMEM((BLOCK, HD), jnp.bfloat16),
            pltpu.VMEM((blocks, VROWS, BLOCK), jnp.bfloat16),
            pltpu.VMEM((2 * HD, width), jnp.bfloat16),
            pltpu.VMEM((8, width), jnp.float32),
            pltpu.VMEM((VROWS, width), jnp.float32),
            pltpu.VMEM(gate_table.shape, jnp.float32),
            pltpu.VMEM((TILES, SPAN, TILE), jnp.bfloat16),
            pltpu.SemaphoreType.DMA((3, NH)),
            pltpu.SemaphoreType.DMA((3, NH)),
            pltpu.SemaphoreType.DMA((8,)),
            pltpu.SemaphoreType.DMA((64,)),
            pltpu.SemaphoreType.DMA((2, blocks)),
            pltpu.SemaphoreType.DMA((24,)),
            pltpu.SemaphoreType.DMA((NH, 3)),
        ],
        compiler_params=pltpu.CompilerParams(
            collective_id=0, has_side_effects=True, vmem_limit_bytes=48 * 2**20
        ),
        cost_estimate=pl.CostEstimate(
            flops=2 * 2 * width * 8192 * HD, bytes_accessed=2**20, transcendentals=width * 8192
        ),
    )(queries, keys, values, fold_map, noisy, noise_step, gate_table)


def solution(mesh):
    placed = (
        P(("ctx", "head"), None),
        P(("ctx", "head"), None),
        P(("ctx", "head"), None),
        P(),
        P(),
        P(),
        P(None, "head"),
    )
    return jax.shard_map(
        local, mesh=mesh, in_specs=placed, out_specs=P(("ctx", "head"), None), check_vma=False
    )
```

```python
import functools
import math

import jax
import jax.numpy as jnp
from jax import lax
from jax.experimental import pallas as pl
from jax.experimental.pallas import tpu as pltpu
from jax.sharding import PartitionSpec as P

HEADS = 48
KVH = 8
HD = 128
SPAN = 128
NZ = 8
NH = 8
RATIO = HEADS // KVH
ROWS = 32
BLOCK = NH * ROWS
GROUP = 4 * BLOCK
FEAT = RATIO * HD
TILE = 256
TILES = 2 * SPAN * RATIO // TILE
VROWS = HD + 16
NEG = -1e30
MESH = pl.DeviceIdType.MESH
K, V = 0, 1


def kernel(
    q_ref, k_ref, v_ref, fold, noisy, noise_step, gate_ref, out_ref,
    q_in, k_buf, v_in, vt_buf, qt, m_s, acc, gate_v, ost,
    a2a_send, a2a_recv, loc_sem, kv_send, kv_recv, out_send, out_recv,
):
    me = lax.axis_index("ctx")
    h = lax.axis_index("head")
    z = lax.div(me, 4)
    x = lax.rem(lax.div(me, 2), 2)
    c = lax.rem(me, 2)
    xh = lax.div(h, 4)
    y = lax.rem(h, 4)

    def ctx_of(dz, x_, c_):
        return lax.rem(z + (dz + NZ), NZ) * 4 + x_ * 2 + c_

    zp, zm = ctx_of(1, x, c), ctx_of(-1, x, c)
    xb, sib = ctx_of(0, 1 - x, c), ctx_of(0, x, 1 - c)
    peers = [(me, xh * 4 + lax.rem(y + r, 4), 4 + lax.rem(y + r, 4), 4 + y) for r in range(1, 4)]
    peers += [(xb, (1 - xh) * 4 + lax.rem(y + r, 4), lax.rem(y + r, 4), y) for r in range(4)]
    mine = 4 + y

    own_k = pltpu.make_async_copy(
        k_ref.at[:, pl.ds(pl.multiple_of(h * HD, HD), HD)],
        k_buf.at[me, pl.ds(pl.multiple_of(mine * ROWS, ROWS), ROWS), :], loc_sem.at[0])
    own_v = pltpu.make_async_copy(
        v_ref.at[:, pl.ds(pl.multiple_of(h * HD, HD), HD)],
        v_in.at[pl.ds(pl.multiple_of(mine * ROWS, ROWS), ROWS), :], loc_sem.at[1])
    own_q = pltpu.make_async_copy(
        q_ref.at[:, pl.ds(pl.multiple_of(h * FEAT, FEAT), FEAT)], q_in.at[mine], loc_sem.at[2])
    gates = pltpu.make_async_copy(gate_ref, gate_v, loc_sem.at[3])
    own_k.start()
    own_v.start()
    own_q.start()
    gates.start()

    barrier = pltpu.get_barrier_semaphore()
    for ctx, head, _, _ in peers:
        pl.semaphore_signal(barrier, inc=1, device_id=(ctx, head), device_id_type=MESH)
    for other in (zp, zm, xb, sib):
        pl.semaphore_signal(barrier, inc=1, device_id=(other, h), device_id_type=MESH)
    vt_buf[:, HD:, :] = jnp.ones((NZ * 4, VROWS - HD, BLOCK), jnp.bfloat16)
    m_s[...] = jnp.full_like(m_s, NEG)
    acc[...] = jnp.zeros_like(acc)
    pl.semaphore_wait(barrier, NH - 1 + 4)

    def k_copy(i, slot, block):
        ctx, head, _, _ = peers[i]
        return pltpu.make_async_remote_copy(
            k_ref.at[:, pl.ds(pl.multiple_of(head * HD, HD), HD)],
            k_buf.at[block, pl.ds(pl.multiple_of(slot * ROWS, ROWS), ROWS), :],
            a2a_send.at[0, i], a2a_recv.at[0, slot], device_id=(ctx, head), device_id_type=MESH)

    def v_copy(i, slot, block):
        ctx, head, _, _ = peers[i]
        return pltpu.make_async_remote_copy(
            v_ref.at[:, pl.ds(pl.multiple_of(head * HD, HD), HD)],
            v_in.at[pl.ds(pl.multiple_of(slot * ROWS, ROWS), ROWS), :],
            a2a_send.at[1, i], a2a_recv.at[1, slot], device_id=(ctx, head), device_id_type=MESH)

    def q_copy(i, slot, block):
        ctx, head, _, _ = peers[i]
        return pltpu.make_async_remote_copy(
            q_ref.at[:, pl.ds(pl.multiple_of(head * FEAT, FEAT), FEAT)], q_in.at[slot],
            a2a_send.at[2, i], a2a_recv.at[2, slot], device_id=(ctx, head), device_id_type=MESH)

    for copy in (k_copy, v_copy, q_copy):
        for i, peer in enumerate(peers):
            copy(i, peer[3], peer[0]).start()

    sent = []

    def block_copy(half, block, target, send):
        ref = k_buf.at[block] if half == K else vt_buf.at[block, pl.ds(0, HD), :]
        return pltpu.make_async_remote_copy(
            ref, ref, kv_send.at[send], kv_recv.at[half, block],
            device_id=(target, h), device_id_type=MESH)

    def send(half, block, *targets):
        for target in targets:
            block_copy(half, block, target, len(sent)).start()
            sent.append((half, block, target))

    def arrived(half, block):
        block_copy(half, block, sib, 0).wait_recv()

    own = lambda d: ctx_of(d, x, c)
    oth = lambda d: ctx_of(d, 1 - x, c)

    def come(half, block, *targets):
        arrived(half, block)
        send(half, block, *targets, sib)

    own_k.wait()
    for i, peer in enumerate(peers):
        k_copy(i, peer[2], me).wait_recv()
    send(K, me, xb, zp, zm, sib)
    own_v.wait()
    for i, peer in enumerate(peers):
        v_copy(i, peer[2], me).wait_recv()
    vt_buf[me, :HD, :] = v_in[...].astype(jnp.float32).T.astype(jnp.bfloat16)
    send(V, me, xb, zp, zm, sib)

    def own_k_came(d):
        come(K, own(-d), zp, xb)
        come(K, own(d), *((zm,) if d < 3 else ()), xb)

    def own_v_came(d):
        come(V, own(-d), *((zp,) if d < 3 else ()))
        come(V, own(d), zm)

    def oth_v_came(d):
        come(V, oth(-d), *((zp,) if d < 3 else ()))
        come(V, oth(d), *((zm,) if d < 3 else ()))

    def sibling(d):
        for x_ in (0, 1):
            for half in (K, V):
                arrived(half, ctx_of(d, x_, 1 - c))

    come(K, oth(0))
    own_k_came(1)
    come(V, oth(0), zp, zm)
    own_v_came(1)

    own_q.wait()
    for i, peer in enumerate(peers):
        q_copy(i, peer[2], me).wait_recv()
    factor = math.log2(math.e) / math.sqrt(HD)
    for slot in range(2):
        for j in range(RATIO):
            part = q_in[slot * 4:slot * 4 + 4, :, j * HD:(j + 1) * HD].reshape(SPAN, HD)
            scaled = (part.astype(jnp.float32) * factor).T
            high = scaled.astype(jnp.bfloat16)
            low = (scaled - high.astype(jnp.float32)).astype(jnp.bfloat16)
            at = (slot * RATIO + j) * HD
            qt[0:HD, at:at + HD] = high
            qt[HD:2 * HD, at:at + HD] = low

    my_order = [fold[2 * xb + 1 - xh], fold[2 * me + xh]]
    gate_rows = [gate_v.at[pl.ds(noise_step[o], 1), :] for o in my_order]
    live = [noisy[o] == 1 for o in my_order]

    def work(zq, slot, done=None):
        keys = k_buf[pl.ds(zq * 4, 4)].reshape(GROUP, HD)
        keys = jnp.concatenate([keys, keys], axis=1)
        values = jnp.concatenate([vt_buf[zq * 4 + i] for i in range(4)], axis=1)
        count = GROUP // SPAN
        first = 8 * zq
        orders = []
        for i in range(4):
            orders.append(fold[first + 2 * ((i + 2) % 4) + 1 - xh])
            orders.append(fold[first + 2 * i + xh])
        slots = (0, 1) if slot is None else (slot,)
        hide = []
        for a in slots:
            order = my_order[a] if isinstance(a, int) else jnp.where(a == 0, my_order[0], my_order[1])
            hide.append([jnp.where(o <= order, jnp.float32(0), jnp.float32(NEG)) for o in orders])
        tiles = (TILES // 2) * len(slots)

        def cols(t):
            if slot is None:
                return slice(t * TILE, (t + 1) * TILE)
            return pl.ds(pl.multiple_of((slot * (TILES // 2) + t) * TILE, TILE), TILE)

        def score(t):
            return jnp.dot(keys, qt[:, cols(t)], preferred_element_type=jnp.float32)

        def soften(t, s):
            bias = hide[t // (TILES // 2)]
            before = m_s[0:1, cols(t)]
            top = before
            for i in range(count):
                top = jnp.maximum(top, jnp.max(s[i * SPAN:(i + 1) * SPAN], axis=0, keepdims=True) + bias[i])
            probs = [
                jnp.exp2(s[i * SPAN:(i + 1) * SPAN] - (top - 2 * bias[i])).astype(jnp.bfloat16)
                for i in range(count)
            ]
            m_s[0:1, cols(t)] = top
            return jnp.concatenate(probs, axis=0), jnp.exp2(before - top)

        def add(t, probs, alpha):
            total = acc[:, cols(t)] * alpha + jnp.dot(values, probs, preferred_element_type=jnp.float32)
            if done is None:
                acc[:, cols(t)] = total
            else:
                done(t, total)

        s = score(0)
        held = None
        for t in range(tiles):
            following = score(t + 1) if t + 1 < tiles else None
            if held is not None:
                add(t - 1, *held)
            held = soften(t, s)
            s = following
        add(tiles - 1, *held)

    events = {
        0: lambda: sibling(0),
        1: lambda: (own_k_came(2), come(K, oth(1))),
        2: lambda: (oth_v_came(1), come(K, oth(-1)), sibling(1), sibling(-1)),
        3: lambda: (own_v_came(2), come(K, oth(2))),
        4: lambda: (own_k_came(3), come(K, oth(-2))),
        5: lambda: oth_v_came(2),
        6: lambda: (sibling(2), sibling(-2)),
        7: lambda: (own_v_came(3), come(K, oth(3))),
        8: lambda: (come(K, own(4), xb), come(K, oth(-3))),
        9: lambda: oth_v_came(3),
        10: lambda: (come(V, own(4), xb), sibling(3), sibling(-3)),
        12: lambda: come(K, oth(4)),
        13: lambda: come(V, oth(4)),
    }

    def step(u, carry):
        for at, todo in events.items():
            @pl.when(u == at)
            def _():
                todo()
        i = lax.div(u, 2)
        near = lax.div(i + 1, 2)
        d = jnp.where(lax.rem(i, 2) == 1, near, NZ - near)
        work(lax.rem(z + d, NZ), lax.rem(u, 2))
        return carry

    lax.fori_loop(0, 2 * (NZ - 1), step, 0)
    sibling(4)

    results = []

    def result_copy(t, part, i):
        jp = t % 3
        ctx, base = (xb, (1 - xh) * 4) if t < 3 else (me, xh * 4)
        return pltpu.make_async_remote_copy(
            ost.at[t, pl.ds(pl.multiple_of(part * ROWS, ROWS), ROWS), :],
            out_ref.at[:, pl.ds(pl.multiple_of(h * FEAT + jp * TILE, TILE), TILE)],
            out_send.at[i], out_recv.at[h, jp],
            device_id=(ctx, base + part), device_id_type=MESH)

    def own_result(t):
        jp = t % 3
        return pltpu.make_async_copy(
            ost.at[t, pl.ds(pl.multiple_of(y * ROWS, ROWS), ROWS), :],
            out_ref.at[:, pl.ds(pl.multiple_of(h * FEAT + jp * TILE, TILE), TILE)],
            loc_sem.at[4 + jp])

    gates.wait()

    def done(t, total):
        slot = t // 3
        jp = t % 3
        scaled = total[:HD] * (1.0 / total[HD:HD + 1])
        for jj in range(2):
            j = 2 * jp + jj
            rows = scaled[:, jj * HD:(jj + 1) * HD].T
            rows = rows * gate_rows[slot][:, j * HD:(j + 1) * HD]
            rows = jnp.where(live[slot], rows, jnp.float32(0))
            ost[t, :, jj * HD:(jj + 1) * HD] = rows.astype(jnp.bfloat16)
        for r in range(4):
            part = lax.rem(y + r, 4)
            if slot == 1 and r == 0:
                own_result(t).start()
                continue
            result_copy(t, part, len(results)).start()
            results.append((t, part))

    work(lax.rem(z + 4, NZ), None, done)

    for jp in range(3):
        own_result(3 + jp).wait()
    for i, (t, part) in enumerate(results):
        result_copy(t, part, i).wait_send()
    for i, peer in enumerate(peers):
        for copy in (k_copy, v_copy, q_copy):
            copy(i, peer[3], peer[0]).wait_send()
    for i, (half, block, target) in enumerate(sent):
        block_copy(half, me, sib, i).wait_send()
    for ctx, head, _, _ in peers:
        for jp in range(3):
            pltpu.make_async_remote_copy(
                ost.at[0, pl.ds(0, ROWS), :],
                out_ref.at[:, pl.ds(pl.multiple_of(head * FEAT + jp * TILE, TILE), TILE)],
                out_send.at[0], out_recv.at[head, jp],
                device_id=(ctx, head), device_id_type=MESH).wait_recv()


def local(queries, keys, values, fold_map, noisy, noise_step, gate_table):
    hbm = pl.BlockSpec(memory_space=pl.ANY)
    smem = pl.BlockSpec(memory_space=pltpu.SMEM)
    width = 2 * SPAN * RATIO
    blocks = NZ * 4
    return pl.pallas_call(
        kernel,
        out_shape=jax.ShapeDtypeStruct(queries.shape, queries.dtype),
        in_specs=[hbm, hbm, hbm, smem, smem, smem, hbm],
        out_specs=hbm,
        scratch_shapes=[
            pltpu.VMEM((NH, ROWS, FEAT), jnp.bfloat16),
            pltpu.VMEM((blocks, BLOCK, HD), jnp.bfloat16),
            pltpu.VMEM((BLOCK, HD), jnp.bfloat16),
            pltpu.VMEM((blocks, VROWS, BLOCK), jnp.bfloat16),
            pltpu.VMEM((2 * HD, width), jnp.bfloat16),
            pltpu.VMEM((8, width), jnp.float32),
            pltpu.VMEM((VROWS, width), jnp.float32),
            pltpu.VMEM(gate_table.shape, jnp.float32),
            pltpu.VMEM((TILES, SPAN, TILE), jnp.bfloat16),
            pltpu.SemaphoreType.DMA((3, NH)),
            pltpu.SemaphoreType.DMA((3, NH)),
            pltpu.SemaphoreType.DMA((8,)),
            pltpu.SemaphoreType.DMA((64,)),
            pltpu.SemaphoreType.DMA((2, blocks)),
            pltpu.SemaphoreType.DMA((24,)),
            pltpu.SemaphoreType.DMA((NH, 3)),
        ],
        compiler_params=pltpu.CompilerParams(
            collective_id=0, has_side_effects=True, vmem_limit_bytes=60 * 2**20
        ),
        cost_estimate=pl.CostEstimate(
            flops=2 * 2 * width * 8192 * HD, bytes_accessed=2**20, transcendentals=width * 8192
        ),
    )(queries, keys, values, fold_map, noisy, noise_step, gate_table)


def solution(mesh):
    placed = (
        P(("ctx", "head"), None),
        P(("ctx", "head"), None),
        P(("ctx", "head"), None),
        P(),
        P(),
        P(),
        P(None, "head"),
    )
    return jax.shard_map(
        local, mesh=mesh, in_specs=placed, out_specs=P(("ctx", "head"), None), check_vma=False
    )
```

```python
import functools
import math

import jax
import jax.numpy as jnp
from jax import lax
from jax.experimental import pallas as pl
from jax.experimental.pallas import tpu as pltpu
from jax.sharding import PartitionSpec as P

HEADS = 48
KVH = 8
HD = 128
SPAN = 128
NZ = 8
NH = 8
RATIO = HEADS // KVH
ROWS = 32
BLOCK = NH * ROWS
GROUP = 4 * BLOCK
FEAT = RATIO * HD
TILE = 256
TILES = 2 * SPAN * RATIO // TILE
VROWS = HD + 16
NEG = -1e30
MESH = pl.DeviceIdType.MESH
K, V = 0, 1


def kernel(
    q_ref, k_ref, v_ref, fold, noisy, noise_step, gate_ref, out_ref,
    q_in, k_loc, v_loc, k_buf, v_in, vt_buf, qt, m_s, acc, gate_v, ost,
    a2a_send, a2a_recv, loc_sem, kv_send, kv_recv, out_send, out_recv,
):
    me = lax.axis_index("ctx")
    h = lax.axis_index("head")
    z = lax.div(me, 4)
    x = lax.rem(lax.div(me, 2), 2)
    c = lax.rem(me, 2)
    xh = lax.div(h, 4)
    y = lax.rem(h, 4)

    def ctx_of(dz, x_, c_):
        return lax.rem(z + (dz + NZ), NZ) * 4 + x_ * 2 + c_

    zp, zm = ctx_of(1, x, c), ctx_of(-1, x, c)
    xb, sib = ctx_of(0, 1 - x, c), ctx_of(0, x, 1 - c)
    peers = [(me, xh * 4 + lax.rem(y + r, 4), 4 + lax.rem(y + r, 4), 4 + y) for r in range(1, 4)]
    peers += [(xb, (1 - xh) * 4 + lax.rem(y + r, 4), lax.rem(y + r, 4), y) for r in range(4)]
    mine = 4 + y

    stage_k = pltpu.make_async_copy(k_ref, k_loc, loc_sem.at[0])
    stage_v = pltpu.make_async_copy(v_ref, v_loc, loc_sem.at[1])
    own_q = pltpu.make_async_copy(
        q_ref.at[:, pl.ds(pl.multiple_of(h * FEAT, FEAT), FEAT)], q_in.at[mine], loc_sem.at[2])
    gates = pltpu.make_async_copy(gate_ref, gate_v, loc_sem.at[3])
    stage_k.start()
    stage_v.start()
    own_q.start()
    gates.start()

    barrier = pltpu.get_barrier_semaphore()
    for ctx, head, _, _ in peers:
        pl.semaphore_signal(barrier, inc=1, device_id=(ctx, head), device_id_type=MESH)
    for other in (zp, zm, xb, sib):
        pl.semaphore_signal(barrier, inc=1, device_id=(other, h), device_id_type=MESH)
    vt_buf[:, HD:, :] = jnp.ones((NZ * 4, VROWS - HD, BLOCK), jnp.bfloat16)
    m_s[...] = jnp.full_like(m_s, NEG)
    acc[...] = jnp.zeros_like(acc)
    stage_k.wait()
    stage_v.wait()
    pl.semaphore_wait(barrier, NH - 1 + 4)

    def k_copy(i, slot, block):
        ctx, head, _, _ = peers[i]
        return pltpu.make_async_remote_copy(
            k_loc.at[:, pl.ds(pl.multiple_of(head * HD, HD), HD)],
            k_buf.at[block, pl.ds(pl.multiple_of(slot * ROWS, ROWS), ROWS), :],
            a2a_send.at[0, i], a2a_recv.at[0, slot], device_id=(ctx, head), device_id_type=MESH)

    def v_copy(i, slot, block):
        ctx, head, _, _ = peers[i]
        return pltpu.make_async_remote_copy(
            v_loc.at[:, pl.ds(pl.multiple_of(head * HD, HD), HD)],
            v_in.at[pl.ds(pl.multiple_of(slot * ROWS, ROWS), ROWS), :],
            a2a_send.at[1, i], a2a_recv.at[1, slot], device_id=(ctx, head), device_id_type=MESH)

    def q_copy(i, slot, block):
        ctx, head, _, _ = peers[i]
        return pltpu.make_async_remote_copy(
            q_ref.at[:, pl.ds(pl.multiple_of(head * FEAT, FEAT), FEAT)], q_in.at[slot],
            a2a_send.at[2, i], a2a_recv.at[2, slot], device_id=(ctx, head), device_id_type=MESH)

    for copy in (k_copy, v_copy, q_copy):
        for i, peer in enumerate(peers):
            copy(i, peer[3], peer[0]).start()
    here = pl.ds(pl.multiple_of(h * HD, HD), HD)
    rows_here = pl.ds(pl.multiple_of(mine * ROWS, ROWS), ROWS)
    k_buf[me, rows_here, :] = k_loc[:, here]
    v_in[rows_here, :] = v_loc[:, here]

    sent = []

    def block_copy(half, block, target, send):
        ref = k_buf.at[block] if half == K else vt_buf.at[block, pl.ds(0, HD), :]
        return pltpu.make_async_remote_copy(
            ref, ref, kv_send.at[send], kv_recv.at[half, block],
            device_id=(target, h), device_id_type=MESH)

    def send(half, block, *targets):
        for target in targets:
            block_copy(half, block, target, len(sent)).start()
            sent.append((half, block, target))

    def arrived(half, block):
        block_copy(half, block, sib, 0).wait_recv()

    own = lambda d: ctx_of(d, x, c)
    oth = lambda d: ctx_of(d, 1 - x, c)

    def come(half, block, *targets):
        arrived(half, block)
        send(half, block, *targets, sib)

    for i, peer in enumerate(peers):
        k_copy(i, peer[2], me).wait_recv()
    send(K, me, xb, zp, zm, sib)
    for i, peer in enumerate(peers):
        v_copy(i, peer[2], me).wait_recv()
    vt_buf[me, :HD, :] = v_in[...].astype(jnp.float32).T.astype(jnp.bfloat16)
    send(V, me, xb, zp, zm, sib)

    def o_k(*ds):
        for d in ds:
            onward = {-1: (zp,), -2: (zp,), -3: (zp,), 1: (zm,), 2: (zm,), 3: (), 4: ()}[d]
            come(K, own(d), *onward, xb)

    def o_v(*ds):
        for d in ds:
            come(V, own(d), *{-1: (zp,), -2: (zp,), -3: (), 1: (zm,), 2: (zm,), 3: (zm,), 4: ()}[d])

    def p_k(*ds):
        for d in ds:
            come(K, oth(d))

    def p_v(*ds):
        for d in ds:
            come(V, oth(d), *{0: (zp, zm), -1: (zp,), -2: (zp,), -3: (zp,), 1: (zm,), 2: (zm,), 3: (), 4: ()}[d])

    def sibling(x_, *ds):
        for d in ds:
            for half in (K, V):
                arrived(half, ctx_of(d, x_, 1 - c))

    p_k(0)
    o_k(-1, 1)
    p_v(0)
    o_v(-1, 1)

    own_q.wait()
    for i, peer in enumerate(peers):
        q_copy(i, peer[2], me).wait_recv()
    factor = math.log2(math.e) / math.sqrt(HD)
    for slot in range(2):
        for j in range(RATIO):
            part = q_in[slot * 4:slot * 4 + 4, :, j * HD:(j + 1) * HD].reshape(SPAN, HD)
            scaled = (part.astype(jnp.float32) * factor).T
            high = scaled.astype(jnp.bfloat16)
            low = (scaled - high.astype(jnp.float32)).astype(jnp.bfloat16)
            at = (slot * RATIO + j) * HD
            qt[0:HD, at:at + HD] = high
            qt[HD:2 * HD, at:at + HD] = low

    my_order = [fold[2 * xb + 1 - xh], fold[2 * me + xh]]
    gate_rows = [gate_v.at[pl.ds(noise_step[o], 1), :] for o in my_order]
    live = [noisy[o] == 1 for o in my_order]

    def group(i):
        away = lax.div(i + 1, 2)
        col_a = jnp.where(lax.rem(i, 2) == 1, x, 1 - x)
        col_b = jnp.where((i == 0) | (i == NZ - 1), 1 - col_a, col_a)
        pairs = []
        for zq, col in ((lax.rem(z + away, NZ), col_a), (lax.rem(z + NZ - away, NZ), col_b)):
            pairs.append((zq * 4 + col * 2, 2 - 4 * col))
        keys = jnp.concatenate([k_buf[pl.ds(b, 2)].reshape(2 * BLOCK, HD) for b, _ in pairs], axis=0)
        keys = jnp.concatenate([keys, keys], axis=1)
        values = jnp.concatenate([vt_buf[b + core] for b, _ in pairs for core in range(2)], axis=1)
        orders = []
        for b, flip in pairs:
            for core in range(2):
                orders.append(fold[2 * (b + core + flip) + 1 - xh])
                orders.append(fold[2 * (b + core) + xh])
        return keys, values, orders

    def work(numbers, slot, done=None):
        order = my_order[slot] if isinstance(slot, int) else jnp.where(slot == 0, my_order[0], my_order[1])
        groups = []
        for i in numbers:
            keys, values, orders = group(i)
            groups.append((keys, values, [jnp.where(o <= order, jnp.float32(0), jnp.float32(NEG)) for o in orders]))
        half = TILES // 2
        units = [(g, t) for g in range(len(groups)) for t in range(half)]

        def cols(t):
            return pl.ds(pl.multiple_of((slot * half + t) * TILE, TILE), TILE)

        def score(g, t):
            return jnp.dot(groups[g][0], qt[:, cols(t)], preferred_element_type=jnp.float32)

        def soften(g, t, s):
            bias = groups[g][2]
            before = m_s[0:1, cols(t)]
            top = before
            for i, b in enumerate(bias):
                top = jnp.maximum(top, jnp.max(s[i * SPAN:(i + 1) * SPAN], axis=0, keepdims=True) + b)
            probs = [
                jnp.exp2(s[i * SPAN:(i + 1) * SPAN] - (top - 2 * b)).astype(jnp.bfloat16)
                for i, b in enumerate(bias)
            ]
            m_s[0:1, cols(t)] = top
            return jnp.concatenate(probs, axis=0), jnp.exp2(before - top)

        def add(g, t, probs, alpha):
            total = acc[:, cols(t)] * alpha + jnp.dot(groups[g][1], probs, preferred_element_type=jnp.float32)
            if done is None or g < len(groups) - 1:
                acc[:, cols(t)] = total
            else:
                done(slot * half + t, total)

        s = score(*units[0])
        held = None
        for n, unit in enumerate(units):
            following = score(*units[n + 1]) if n + 1 < len(units) else None
            if held is not None:
                add(*units[n - 1], *held)
            held = soften(*unit, s)
            s = following
        add(*units[-1], *held)

    events = {
        0: lambda: (sibling(x, 0), sibling(1 - x, 0)),
        1: lambda: (o_k(-2, 2), p_k(-1)),
        2: lambda: (p_k(1), p_v(-1, 1), sibling(x, -1, 1)),
        3: lambda: o_v(-2, 2),
        4: lambda: (p_k(-2), sibling(1 - x, -1, 1)),
        5: lambda: (o_k(-3, 3), p_k(2)),
        6: lambda: (p_v(-2, 2), sibling(x, -2, 2)),
        7: lambda: o_v(-3, 3),
        8: lambda: sibling(1 - x, -2, 2),
        9: lambda: (o_k(4), p_k(-3)),
        10: lambda: (p_v(-3, 3), p_k(3), sibling(x, -3, 3)),
        11: lambda: o_v(4),
        12: lambda: (p_k(4), sibling(1 - x, -3, 3)),
    }

    def step(u, carry):
        for at, todo in events.items():
            @pl.when(u == at)
            def _():
                todo()
        work([lax.div(u, 2)], lax.rem(u, 2))
        return carry

    lax.fori_loop(0, 2 * NZ - 3, step, 0)
    p_v(4)
    sibling(x, 4)
    sibling(1 - x, 4)

    results = []

    def result_copy(t, part, i):
        jp = t % 3
        ctx, base = (xb, (1 - xh) * 4) if t < 3 else (me, xh * 4)
        return pltpu.make_async_remote_copy(
            ost.at[t, pl.ds(pl.multiple_of(part * ROWS, ROWS), ROWS), :],
            out_ref.at[:, pl.ds(pl.multiple_of(h * FEAT + jp * TILE, TILE), TILE)],
            out_send.at[i], out_recv.at[h, jp],
            device_id=(ctx, base + part), device_id_type=MESH)

    def own_result(t):
        jp = t % 3
        return pltpu.make_async_copy(
            ost.at[t, pl.ds(pl.multiple_of(y * ROWS, ROWS), ROWS), :],
            out_ref.at[:, pl.ds(pl.multiple_of(h * FEAT + jp * TILE, TILE), TILE)],
            loc_sem.at[4 + jp])

    gates.wait()

    def done(t, total):
        slot = t // 3
        jp = t % 3
        scaled = total[:HD] * (1.0 / total[HD:HD + 1])
        for jj in range(2):
            j = 2 * jp + jj
            rows = scaled[:, jj * HD:(jj + 1) * HD].T
            rows = rows * gate_rows[slot][:, j * HD:(j + 1) * HD]
            rows = jnp.where(live[slot], rows, jnp.float32(0))
            ost[t, :, jj * HD:(jj + 1) * HD] = rows.astype(jnp.bfloat16)
        for r in range(4):
            part = lax.rem(y + r, 4)
            if slot == 1 and r == 0:
                own_result(t).start()
                continue
            result_copy(t, part, len(results)).start()
            results.append((t, part))

    work([NZ - 1], 0, done)
    work([NZ - 2, NZ - 1], 1, done)

    for jp in range(3):
        own_result(3 + jp).wait()
    for i, (t, part) in enumerate(results):
        result_copy(t, part, i).wait_send()
    for i, peer in enumerate(peers):
        for copy in (k_copy, v_copy, q_copy):
            copy(i, peer[3], peer[0]).wait_send()
    for i, (half, block, target) in enumerate(sent):
        block_copy(half, me, sib, i).wait_send()
    for ctx, head, _, _ in peers:
        for jp in range(3):
            pltpu.make_async_remote_copy(
                ost.at[0, pl.ds(0, ROWS), :],
                out_ref.at[:, pl.ds(pl.multiple_of(head * FEAT + jp * TILE, TILE), TILE)],
                out_send.at[0], out_recv.at[head, jp],
                device_id=(ctx, head), device_id_type=MESH).wait_recv()


def local(queries, keys, values, fold_map, noisy, noise_step, gate_table):
    hbm = pl.BlockSpec(memory_space=pl.ANY)
    smem = pl.BlockSpec(memory_space=pltpu.SMEM)
    width = 2 * SPAN * RATIO
    blocks = NZ * 4
    return pl.pallas_call(
        kernel,
        out_shape=jax.ShapeDtypeStruct(queries.shape, queries.dtype),
        in_specs=[hbm, hbm, hbm, smem, smem, smem, hbm],
        out_specs=hbm,
        scratch_shapes=[
            pltpu.VMEM((NH, ROWS, FEAT), jnp.bfloat16),
            pltpu.VMEM(keys.shape, jnp.bfloat16),
            pltpu.VMEM(values.shape, jnp.bfloat16),
            pltpu.VMEM((blocks, BLOCK, HD), jnp.bfloat16),
            pltpu.VMEM((BLOCK, HD), jnp.bfloat16),
            pltpu.VMEM((blocks, VROWS, BLOCK), jnp.bfloat16),
            pltpu.VMEM((2 * HD, width), jnp.bfloat16),
            pltpu.VMEM((8, width), jnp.float32),
            pltpu.VMEM((VROWS, width), jnp.float32),
            pltpu.VMEM(gate_table.shape, jnp.float32),
            pltpu.VMEM((TILES, SPAN, TILE), jnp.bfloat16),
            pltpu.SemaphoreType.DMA((3, NH)),
            pltpu.SemaphoreType.DMA((3, NH)),
            pltpu.SemaphoreType.DMA((8,)),
            pltpu.SemaphoreType.DMA((64,)),
            pltpu.SemaphoreType.DMA((2, blocks)),
            pltpu.SemaphoreType.DMA((24,)),
            pltpu.SemaphoreType.DMA((NH, 3)),
        ],
        compiler_params=pltpu.CompilerParams(
            collective_id=0, has_side_effects=True, vmem_limit_bytes=60 * 2**20
        ),
        cost_estimate=pl.CostEstimate(
            flops=2 * 2 * width * 8192 * HD, bytes_accessed=2**20, transcendentals=width * 8192
        ),
    )(queries, keys, values, fold_map, noisy, noise_step, gate_table)


def solution(mesh):
    placed = (
        P(("ctx", "head"), None),
        P(("ctx", "head"), None),
        P(("ctx", "head"), None),
        P(),
        P(),
        P(),
        P(None, "head"),
    )
    return jax.shard_map(
        local, mesh=mesh, in_specs=placed, out_specs=P(("ctx", "head"), None), check_vma=False
    )
```

```python
import functools
import math

import jax
import jax.numpy as jnp
from jax import lax
from jax.experimental import pallas as pl
from jax.experimental.pallas import tpu as pltpu
from jax.sharding import PartitionSpec as P

HEADS = 48
KVH = 8
HD = 128
SPAN = 128
NZ = 8
NH = 8
RATIO = HEADS // KVH
ROWS = 32
BLOCK = NH * ROWS
GROUP = 4 * BLOCK
FEAT = RATIO * HD
TILE = 256
TILES = 2 * SPAN * RATIO // TILE
VROWS = HD + 16
NEG = -1e30
MESH = pl.DeviceIdType.MESH
K, V = 0, 1


def kernel(
    q_ref, k_ref, v_ref, fold, noisy, noise_step, gate_ref, out_ref,
    q_in, k_loc, v_loc, k_buf, v_in, vt_buf, qt, m_s, acc, gate_v, ost,
    a2a_send, a2a_recv, loc_sem, kv_send, kv_recv, out_send, out_recv,
):
    me = lax.axis_index("ctx")
    h = lax.axis_index("head")
    z = lax.div(me, 4)
    x = lax.rem(lax.div(me, 2), 2)
    c = lax.rem(me, 2)
    xh = lax.div(h, 4)
    y = lax.rem(h, 4)

    def ctx_of(dz, x_, c_):
        return lax.rem(z + (dz + NZ), NZ) * 4 + x_ * 2 + c_

    zp, zm = ctx_of(1, x, c), ctx_of(-1, x, c)
    xb, sib = ctx_of(0, 1 - x, c), ctx_of(0, x, 1 - c)
    peers = [(me, xh * 4 + lax.rem(y + r, 4), 4 + lax.rem(y + r, 4), 4 + y) for r in range(1, 4)]
    peers += [(xb, (1 - xh) * 4 + lax.rem(y + r, 4), lax.rem(y + r, 4), y) for r in range(4)]
    mine = 4 + y

    stage_k = pltpu.make_async_copy(k_ref, k_loc, loc_sem.at[0])
    stage_v = pltpu.make_async_copy(v_ref, v_loc, loc_sem.at[1])
    own_q = pltpu.make_async_copy(
        q_ref.at[:, pl.ds(pl.multiple_of(h * FEAT, FEAT), FEAT)], q_in.at[mine], loc_sem.at[2])
    gates = pltpu.make_async_copy(gate_ref, gate_v, loc_sem.at[3])
    stage_k.start()
    stage_v.start()
    own_q.start()
    gates.start()

    barrier = pltpu.get_barrier_semaphore()
    for ctx, head, _, _ in peers:
        pl.semaphore_signal(barrier, inc=1, device_id=(ctx, head), device_id_type=MESH)
    for other in (zp, zm, xb, sib):
        pl.semaphore_signal(barrier, inc=1, device_id=(other, h), device_id_type=MESH)
    vt_buf[:, HD:, :] = jnp.ones((NZ * 4, VROWS - HD, BLOCK), jnp.bfloat16)
    m_s[...] = jnp.full_like(m_s, NEG)
    acc[...] = jnp.zeros_like(acc)
    stage_k.wait()
    stage_v.wait()
    pl.semaphore_wait(barrier, NH - 1 + 4)

    def k_copy(i, slot, block):
        ctx, head, _, _ = peers[i]
        return pltpu.make_async_remote_copy(
            k_loc.at[:, pl.ds(pl.multiple_of(head * HD, HD), HD)],
            k_buf.at[block, pl.ds(pl.multiple_of(slot * ROWS, ROWS), ROWS), :],
            a2a_send.at[0, i], a2a_recv.at[0, slot], device_id=(ctx, head), device_id_type=MESH)

    def v_copy(i, slot, block):
        ctx, head, _, _ = peers[i]
        return pltpu.make_async_remote_copy(
            v_loc.at[:, pl.ds(pl.multiple_of(head * HD, HD), HD)],
            v_in.at[pl.ds(pl.multiple_of(slot * ROWS, ROWS), ROWS), :],
            a2a_send.at[1, i], a2a_recv.at[1, slot], device_id=(ctx, head), device_id_type=MESH)

    def q_copy(i, slot, block):
        ctx, head, _, _ = peers[i]
        return pltpu.make_async_remote_copy(
            q_ref.at[:, pl.ds(pl.multiple_of(head * FEAT, FEAT), FEAT)], q_in.at[slot],
            a2a_send.at[2, i], a2a_recv.at[2, slot], device_id=(ctx, head), device_id_type=MESH)

    for copy in (k_copy, v_copy, q_copy):
        for i, peer in enumerate(peers):
            copy(i, peer[3], peer[0]).start()
    here = pl.ds(pl.multiple_of(h * HD, HD), HD)
    rows_here = pl.ds(pl.multiple_of(mine * ROWS, ROWS), ROWS)
    k_buf[me, rows_here, :] = k_loc[:, here]
    v_in[rows_here, :] = v_loc[:, here]

    sent = []
    targets = dict(zp=zp, zm=zm, xb=xb, sib=sib)
    links = list(targets)

    def block_of(column, d, core):
        return ctx_of(d, x if column == 0 else 1 - x, core)

    def block_copy(half, block, link, column, d):
        ref = k_buf.at[block] if half == K else vt_buf.at[block, pl.ds(0, HD), :]
        return pltpu.make_async_remote_copy(
            ref, ref, kv_send.at[links.index(link), half, column * NZ + lax.rem(d + NZ, NZ)],
            kv_recv.at[half, block], device_id=(targets[link], h), device_id_type=MESH)

    def send(half, column, d, *onto, ds=None):
        for link in onto:
            block_copy(half, block_of(column, d, c), link, column, d).start()
            for value in (d,) if ds is None else ds:
                sent.append((half, column, value, link))

    def arrived(half, column, d, core=c):
        block_copy(half, block_of(column, d, core), "sib", column, d).wait_recv()

    def come(half, column, d, *onto, ds=None):
        arrived(half, column, d)
        send(half, column, d, *onto, "sib", ds=ds)

    def sibling(column, *steps):
        for d in steps:
            for half in (K, V):
                arrived(half, column, d, 1 - c)

    for i, peer in enumerate(peers):
        k_copy(i, peer[2], me).wait_recv()
    send(K, 0, 0, *links)
    for i, peer in enumerate(peers):
        v_copy(i, peer[2], me).wait_recv()
    vt_buf[me, :HD, :] = v_in[...].astype(jnp.float32).T.astype(jnp.bfloat16)
    send(V, 0, 0, *links)

    come(K, 1, 0)
    come(K, 0, -1, "zp", "xb")
    come(K, 0, 1, "zm", "xb")
    come(V, 1, 0, "zp", "zm")
    come(V, 0, -1, "zp")
    come(V, 0, 1, "zm")

    own_q.wait()
    for i, peer in enumerate(peers):
        q_copy(i, peer[2], me).wait_recv()
    factor = math.log2(math.e) / math.sqrt(HD)
    for slot in range(2):
        for j in range(RATIO):
            part = q_in[slot * 4:slot * 4 + 4, :, j * HD:(j + 1) * HD].reshape(SPAN, HD)
            scaled = (part.astype(jnp.float32) * factor).T
            high = scaled.astype(jnp.bfloat16)
            low = (scaled - high.astype(jnp.float32)).astype(jnp.bfloat16)
            at = (slot * RATIO + j) * HD
            qt[0:HD, at:at + HD] = high
            qt[HD:2 * HD, at:at + HD] = low

    my_order = [fold[2 * xb + 1 - xh], fold[2 * me + xh]]
    gate_rows = [gate_v.at[pl.ds(noise_step[o], 1), :] for o in my_order]
    live = [noisy[o] == 1 for o in my_order]

    def group(i):
        away = lax.div(i + 1, 2)
        col_a = jnp.where(lax.rem(i, 2) == 1, x, 1 - x)
        col_b = jnp.where((i == 0) | (i == NZ - 1), 1 - col_a, col_a)
        pairs = []
        for zq, col in ((lax.rem(z + away, NZ), col_a), (lax.rem(z + NZ - away, NZ), col_b)):
            pairs.append((zq * 4 + col * 2, 2 - 4 * col))
        keys = jnp.concatenate([k_buf[pl.ds(b, 2)].reshape(2 * BLOCK, HD) for b, _ in pairs], axis=0)
        keys = jnp.concatenate([keys, keys], axis=1)
        values = jnp.concatenate([vt_buf[b + core] for b, _ in pairs for core in range(2)], axis=1)
        orders = []
        for b, flip in pairs:
            for core in range(2):
                orders.append(fold[2 * (b + core + flip) + 1 - xh])
                orders.append(fold[2 * (b + core) + xh])
        return keys, values, orders

    def work(numbers, slot, done=None):
        order = my_order[slot] if isinstance(slot, int) else jnp.where(slot == 0, my_order[0], my_order[1])
        groups = []
        for i in numbers:
            keys, values, orders = group(i)
            groups.append((keys, values, [jnp.where(o <= order, jnp.float32(0), jnp.float32(NEG)) for o in orders]))
        half = TILES // 2
        units = [(g, t) for g in range(len(groups)) for t in range(half)]

        def cols(t):
            return pl.ds(pl.multiple_of((slot * half + t) * TILE, TILE), TILE)

        def score(g, t):
            return jnp.dot(groups[g][0], qt[:, cols(t)], preferred_element_type=jnp.float32)

        def soften(g, t, s):
            bias = groups[g][2]
            before = m_s[0:1, cols(t)]
            top = before
            for i, b in enumerate(bias):
                top = jnp.maximum(top, jnp.max(s[i * SPAN:(i + 1) * SPAN], axis=0, keepdims=True) + b)
            probs = [
                jnp.exp2(s[i * SPAN:(i + 1) * SPAN] - (top - 2 * b)).astype(jnp.bfloat16)
                for i, b in enumerate(bias)
            ]
            m_s[0:1, cols(t)] = top
            return jnp.concatenate(probs, axis=0), jnp.exp2(before - top)

        def add(g, t, probs, alpha):
            total = acc[:, cols(t)] * alpha + jnp.dot(groups[g][1], probs, preferred_element_type=jnp.float32)
            if done is None or g < len(groups) - 1:
                acc[:, cols(t)] = total
            else:
                done(slot * half + t, total)

        s = score(*units[0])
        held = None
        for n, unit in enumerate(units):
            following = score(*units[n + 1]) if n + 1 < len(units) else None
            if held is not None:
                add(*units[n - 1], *held)
            held = soften(*unit, s)
            s = following
        add(*units[-1], *held)

    def round_of(d, carry):
        @pl.when(d == 1)
        def _():
            sibling(0, 0)
            sibling(1, 0)

        @pl.when(d > 1)
        def _():
            sibling(1, 1 - d, d - 1)

        work([2 * d - 2], 0)

        @pl.when(d < 3)
        def _():
            come(K, 0, -d - 1, "zp", "xb", ds=(-2, -3))

        arrived(K, 0, d + 1)

        @pl.when(d == 1)
        def _():
            send(K, 0, d + 1, "zm", ds=(2,))

        send(K, 0, d + 1, "xb", "sib", ds=(2, 3, 4))
        come(K, 1, -d, ds=(-1, -2, -3))
        work([2 * d - 2], 1)

        come(K, 1, d, ds=(1, 2, 3))
        come(V, 1, -d, "zp", ds=(-1, -2, -3))
        arrived(V, 1, d)

        @pl.when(d < 3)
        def _():
            send(V, 1, d, "zm", ds=(1, 2))

        send(V, 1, d, "sib", ds=(1, 2, 3))
        sibling(0, -d, d)
        work([2 * d - 1], 0)

        @pl.when(d < 3)
        def _():
            arrived(V, 0, -d - 1)

        @pl.when(d == 1)
        def _():
            send(V, 0, -d - 1, "zp", ds=(-2,))

        @pl.when(d < 3)
        def _():
            send(V, 0, -d - 1, "sib", ds=(-2, -3))

        arrived(V, 0, d + 1)

        @pl.when(d < 3)
        def _():
            send(V, 0, d + 1, "zm", ds=(2, 3))

        send(V, 0, d + 1, "sib", ds=(2, 3, 4))

        @pl.when(d == 3)
        def _():
            sibling(1, -d, d)

        work([jnp.where(d == 3, NZ - 2, 2 * d - 1)], jnp.where(d == 3, 0, 1))
        return carry

    lax.fori_loop(1, 4, round_of, 0)
    come(K, 1, 4)
    come(V, 1, 4)
    sibling(0, 4)
    sibling(1, 4)

    results = []

    def result_copy(t, part, i):
        jp = t % 3
        ctx, base = (xb, (1 - xh) * 4) if t < 3 else (me, xh * 4)
        return pltpu.make_async_remote_copy(
            ost.at[t, pl.ds(pl.multiple_of(part * ROWS, ROWS), ROWS), :],
            out_ref.at[:, pl.ds(pl.multiple_of(h * FEAT + jp * TILE, TILE), TILE)],
            out_send.at[i], out_recv.at[h, jp],
            device_id=(ctx, base + part), device_id_type=MESH)

    def own_result(t):
        jp = t % 3
        return pltpu.make_async_copy(
            ost.at[t, pl.ds(pl.multiple_of(y * ROWS, ROWS), ROWS), :],
            out_ref.at[:, pl.ds(pl.multiple_of(h * FEAT + jp * TILE, TILE), TILE)],
            loc_sem.at[4 + jp])

    gates.wait()

    def done(t, total):
        slot = t // 3
        jp = t % 3
        scaled = total[:HD] * (1.0 / total[HD:HD + 1])
        for jj in range(2):
            j = 2 * jp + jj
            rows = scaled[:, jj * HD:(jj + 1) * HD].T
            rows = rows * gate_rows[slot][:, j * HD:(j + 1) * HD]
            rows = jnp.where(live[slot], rows, jnp.float32(0))
            ost[t, :, jj * HD:(jj + 1) * HD] = rows.astype(jnp.bfloat16)
        for r in range(4):
            part = lax.rem(y + r, 4)
            if slot == 1 and r == 0:
                own_result(t).start()
                continue
            result_copy(t, part, len(results)).start()
            results.append((t, part))

    work([NZ - 1], 0, done)
    work([NZ - 3, NZ - 2, NZ - 1], 1, done)

    for jp in range(3):
        own_result(3 + jp).wait()
    for i, (t, part) in enumerate(results):
        result_copy(t, part, i).wait_send()
    for i, peer in enumerate(peers):
        for copy in (k_copy, v_copy, q_copy):
            copy(i, peer[3], peer[0]).wait_send()
    for half, column, d, link in sent:
        block_copy(half, me, link, column, d).wait_send()
    for ctx, head, _, _ in peers:
        for jp in range(3):
            pltpu.make_async_remote_copy(
                ost.at[0, pl.ds(0, ROWS), :],
                out_ref.at[:, pl.ds(pl.multiple_of(head * FEAT + jp * TILE, TILE), TILE)],
                out_send.at[0], out_recv.at[head, jp],
                device_id=(ctx, head), device_id_type=MESH).wait_recv()


def local(queries, keys, values, fold_map, noisy, noise_step, gate_table):
    hbm = pl.BlockSpec(memory_space=pl.ANY)
    smem = pl.BlockSpec(memory_space=pltpu.SMEM)
    width = 2 * SPAN * RATIO
    blocks = NZ * 4
    return pl.pallas_call(
        kernel,
        out_shape=jax.ShapeDtypeStruct(queries.shape, queries.dtype),
        in_specs=[hbm, hbm, hbm, smem, smem, smem, hbm],
        out_specs=hbm,
        scratch_shapes=[
            pltpu.VMEM((NH, ROWS, FEAT), jnp.bfloat16),
            pltpu.VMEM(keys.shape, jnp.bfloat16),
            pltpu.VMEM(values.shape, jnp.bfloat16),
            pltpu.VMEM((blocks, BLOCK, HD), jnp.bfloat16),
            pltpu.VMEM((BLOCK, HD), jnp.bfloat16),
            pltpu.VMEM((blocks, VROWS, BLOCK), jnp.bfloat16),
            pltpu.VMEM((2 * HD, width), jnp.bfloat16),
            pltpu.VMEM((8, width), jnp.float32),
            pltpu.VMEM((VROWS, width), jnp.float32),
            pltpu.VMEM(gate_table.shape, jnp.float32),
            pltpu.VMEM((TILES, SPAN, TILE), jnp.bfloat16),
            pltpu.SemaphoreType.DMA((3, NH)),
            pltpu.SemaphoreType.DMA((3, NH)),
            pltpu.SemaphoreType.DMA((8,)),
            pltpu.SemaphoreType.DMA((4, 2, 2 * NZ)),
            pltpu.SemaphoreType.DMA((2, blocks)),
            pltpu.SemaphoreType.DMA((24,)),
            pltpu.SemaphoreType.DMA((NH, 3)),
        ],
        compiler_params=pltpu.CompilerParams(
            collective_id=0, has_side_effects=True, vmem_limit_bytes=60 * 2**20
        ),
        cost_estimate=pl.CostEstimate(
            flops=2 * 2 * width * 8192 * HD, bytes_accessed=2**20, transcendentals=width * 8192
        ),
    )(queries, keys, values, fold_map, noisy, noise_step, gate_table)


def solution(mesh):
    placed = (
        P(("ctx", "head"), None),
        P(("ctx", "head"), None),
        P(("ctx", "head"), None),
        P(),
        P(),
        P(),
        P(None, "head"),
    )
    return jax.shard_map(
        local, mesh=mesh, in_specs=placed, out_specs=P(("ctx", "head"), None), check_vma=False
    )
```

```python
import functools
import math

import jax
import jax.numpy as jnp
from jax import lax
from jax.experimental import pallas as pl
from jax.experimental.pallas import tpu as pltpu
from jax.sharding import PartitionSpec as P

HEADS = 48
KVH = 8
HD = 128
SPAN = 128
NZ = 8
NH = 8
RATIO = HEADS // KVH
ROWS = 32
BLOCK = NH * ROWS
GROUP = 4 * BLOCK
FEAT = RATIO * HD
TILE = 256
TILES = 2 * SPAN * RATIO // TILE
VROWS = HD + 16
NEG = -1e30
MESH = pl.DeviceIdType.MESH
K, V = 0, 1


def kernel(
    q_ref, k_ref, v_ref, fold, noisy, noise_step, gate_ref, out_ref,
    q_in, k_loc, v_loc, k_buf, v_in, vt_buf, qt, m_s, acc, gate_v, ost,
    a2a_send, a2a_recv, loc_sem, kv_send, kv_recv, out_send, out_recv,
):
    me = lax.axis_index("ctx")
    h = lax.axis_index("head")
    z = lax.div(me, 4)
    x = lax.rem(lax.div(me, 2), 2)
    c = lax.rem(me, 2)
    xh = lax.div(h, 4)
    y = lax.rem(h, 4)

    def ctx_of(dz, x_, c_):
        return lax.rem(z + (dz + NZ), NZ) * 4 + x_ * 2 + c_

    zp, zm = ctx_of(1, x, c), ctx_of(-1, x, c)
    xb, sib = ctx_of(0, 1 - x, c), ctx_of(0, x, 1 - c)
    peers = [(me, xh * 4 + lax.rem(y + r, 4), 4 + lax.rem(y + r, 4), 4 + y) for r in range(1, 4)]
    peers += [(xb, (1 - xh) * 4 + lax.rem(y + r, 4), lax.rem(y + r, 4), y) for r in range(4)]
    mine = 4 + y

    stage_k = pltpu.make_async_copy(k_ref, k_loc, loc_sem.at[0])
    stage_v = pltpu.make_async_copy(v_ref, v_loc, loc_sem.at[1])
    own_q = pltpu.make_async_copy(
        q_ref.at[:, pl.ds(pl.multiple_of(h * FEAT, FEAT), FEAT)], q_in.at[mine], loc_sem.at[2])
    gates = pltpu.make_async_copy(gate_ref, gate_v, loc_sem.at[3])
    stage_k.start()
    stage_v.start()
    own_q.start()
    gates.start()

    barrier = pltpu.get_barrier_semaphore()
    for ctx, head, _, _ in peers:
        pl.semaphore_signal(barrier, inc=1, device_id=(ctx, head), device_id_type=MESH)
    for other in (zp, zm, xb, sib):
        pl.semaphore_signal(barrier, inc=1, device_id=(other, h), device_id_type=MESH)
    vt_buf[:, HD:, :] = jnp.ones((NZ * 4, VROWS - HD, BLOCK), jnp.bfloat16)
    m_s[...] = jnp.full_like(m_s, NEG)
    acc[...] = jnp.zeros_like(acc)
    stage_k.wait()
    stage_v.wait()
    pl.semaphore_wait(barrier, NH - 1 + 4)

    def k_copy(i, slot, block):
        ctx, head, _, _ = peers[i]
        return pltpu.make_async_remote_copy(
            k_loc.at[:, pl.ds(pl.multiple_of(head * HD, HD), HD)],
            k_buf.at[block, pl.ds(pl.multiple_of(slot * ROWS, ROWS), ROWS), :],
            a2a_send.at[0, i], a2a_recv.at[0, slot], device_id=(ctx, head), device_id_type=MESH)

    def v_copy(i, slot, block):
        ctx, head, _, _ = peers[i]
        return pltpu.make_async_remote_copy(
            v_loc.at[:, pl.ds(pl.multiple_of(head * HD, HD), HD)],
            v_in.at[pl.ds(pl.multiple_of(slot * ROWS, ROWS), ROWS), :],
            a2a_send.at[1, i], a2a_recv.at[1, slot], device_id=(ctx, head), device_id_type=MESH)

    def q_copy(i, slot, block):
        ctx, head, _, _ = peers[i]
        return pltpu.make_async_remote_copy(
            q_ref.at[:, pl.ds(pl.multiple_of(head * FEAT, FEAT), FEAT)], q_in.at[slot],
            a2a_send.at[2, i], a2a_recv.at[2, slot], device_id=(ctx, head), device_id_type=MESH)

    for copy in (k_copy, v_copy, q_copy):
        for i, peer in enumerate(peers):
            copy(i, peer[3], peer[0]).start()
    here = pl.ds(pl.multiple_of(h * HD, HD), HD)
    rows_here = pl.ds(pl.multiple_of(mine * ROWS, ROWS), ROWS)
    k_buf[me, rows_here, :] = k_loc[:, here]
    v_in[rows_here, :] = v_loc[:, here]

    sent = []
    targets = dict(zp=zp, zm=zm, xb=xb, sib=sib)
    links = list(targets)

    def block_of(column, d, core):
        return ctx_of(d, x if column == 0 else 1 - x, core)

    def block_copy(half, block, link, column, d):
        ref = k_buf.at[block] if half == K else vt_buf.at[block, pl.ds(0, HD), :]
        return pltpu.make_async_remote_copy(
            ref, ref, kv_send.at[links.index(link), half, column * NZ + lax.rem(d + NZ, NZ)],
            kv_recv.at[half, block], device_id=(targets[link], h), device_id_type=MESH)

    def send(half, column, d, *onto, ds=None):
        for link in onto:
            block_copy(half, block_of(column, d, c), link, column, d).start()
            for value in (d,) if ds is None else ds:
                sent.append((half, column, value, link))

    def arrived(half, column, d, core=c):
        block_copy(half, block_of(column, d, core), "sib", column, d).wait_recv()

    def come(half, column, d, *onto, ds=None):
        arrived(half, column, d)
        send(half, column, d, *onto, "sib", ds=ds)

    def sibling(column, *steps):
        for d in steps:
            for half in (K, V):
                arrived(half, column, d, 1 - c)

    for i, peer in enumerate(peers):
        k_copy(i, peer[2], me).wait_recv()
    send(K, 0, 0, *links)
    for i, peer in enumerate(peers):
        v_copy(i, peer[2], me).wait_recv()
    vt_buf[me, :HD, :] = v_in[...].astype(jnp.float32).T.astype(jnp.bfloat16)
    send(V, 0, 0, *links)

    come(K, 1, 0)
    come(K, 0, -1, "zp", "xb")
    come(K, 0, 1, "zm", "xb")
    come(V, 1, 0, "zp", "zm")
    come(V, 0, -1, "zp")
    come(V, 0, 1, "zm")

    own_q.wait()
    for i, peer in enumerate(peers):
        q_copy(i, peer[2], me).wait_recv()
    factor = math.log2(math.e) / math.sqrt(HD)
    for slot in range(2):
        for j in range(RATIO):
            part = q_in[slot * 4:slot * 4 + 4, :, j * HD:(j + 1) * HD].reshape(SPAN, HD)
            scaled = (part.astype(jnp.float32) * factor).T
            high = scaled.astype(jnp.bfloat16)
            low = (scaled - high.astype(jnp.float32)).astype(jnp.bfloat16)
            at = (slot * RATIO + j) * HD
            qt[0:HD, at:at + HD] = high
            qt[HD:2 * HD, at:at + HD] = low

    my_order = [fold[2 * xb + 1 - xh], fold[2 * me + xh]]
    gate_rows = [gate_v.at[pl.ds(noise_step[o], 1), :] for o in my_order]
    live = [noisy[o] == 1 for o in my_order]

    def group(i):
        away = lax.div(i + 1, 2)
        col_a = jnp.where(lax.rem(i, 2) == 1, x, 1 - x)
        col_b = jnp.where((i == 0) | (i == NZ - 1), 1 - col_a, col_a)
        pairs = []
        for zq, col in ((lax.rem(z + away, NZ), col_a), (lax.rem(z + NZ - away, NZ), col_b)):
            pairs.append((zq * 4 + col * 2, 2 - 4 * col))
        keys = jnp.concatenate([k_buf[pl.ds(b, 2)].reshape(2 * BLOCK, HD) for b, _ in pairs], axis=0)
        keys = jnp.concatenate([keys, keys], axis=1)
        values = jnp.concatenate([vt_buf[b + core] for b, _ in pairs for core in range(2)], axis=1)
        orders = []
        for b, flip in pairs:
            for core in range(2):
                orders.append(fold[2 * (b + core + flip) + 1 - xh])
                orders.append(fold[2 * (b + core) + xh])
        return keys, values, orders

    def work(*parts):
        half = TILES // 2
        units = [(p, t) for p in range(len(parts)) for t in range(half)]
        groups = {}

        def enter(p):
            before, number, slot, _ = parts[p]
            if before is not None:
                before()
            order = my_order[slot] if isinstance(slot, int) else jnp.where(slot == 0, my_order[0], my_order[1])
            keys, values, orders = group(number)
            groups[p] = keys, values, [jnp.where(o <= order, jnp.float32(0), jnp.float32(NEG)) for o in orders]

        def cols(p, t):
            return pl.ds(pl.multiple_of((parts[p][2] * half + t) * TILE, TILE), TILE)

        def score(p, t):
            if p not in groups:
                enter(p)
            return jnp.dot(groups[p][0], qt[:, cols(p, t)], preferred_element_type=jnp.float32)

        def soften(p, t, s):
            bias = groups[p][2]
            before = m_s[0:1, cols(p, t)]
            top = before
            for i, b in enumerate(bias):
                top = jnp.maximum(top, jnp.max(s[i * SPAN:(i + 1) * SPAN], axis=0, keepdims=True) + b)
            probs = [
                jnp.exp2(s[i * SPAN:(i + 1) * SPAN] - (top - 2 * b)).astype(jnp.bfloat16)
                for i, b in enumerate(bias)
            ]
            m_s[0:1, cols(p, t)] = top
            return jnp.concatenate(probs, axis=0), jnp.exp2(before - top)

        def add(p, t, probs, alpha):
            total = acc[:, cols(p, t)] * alpha + jnp.dot(groups[p][1], probs, preferred_element_type=jnp.float32)
            if parts[p][3] is None:
                acc[:, cols(p, t)] = total
            else:
                parts[p][3](parts[p][2] * half + t, total)

        s = score(*units[0])
        held = None
        for n, unit in enumerate(units):
            following = score(*units[n + 1]) if n + 1 < len(units) else None
            if held is not None:
                add(*units[n - 1], *held)
            held = soften(*unit, s)
            s = following
        add(*units[-1], *held)

    def round_of(d, carry):
        def first():
            @pl.when(d == 1)
            def _():
                sibling(0, 0)
                sibling(1, 0)

            @pl.when(d > 1)
            def _():
                sibling(1, 1 - d, d - 1)

        def second():
            @pl.when(d < 3)
            def _():
                come(K, 0, -d - 1, "zp", "xb", ds=(-2, -3))

            arrived(K, 0, d + 1)

            @pl.when(d == 1)
            def _():
                send(K, 0, d + 1, "zm", ds=(2,))

            send(K, 0, d + 1, "xb", "sib", ds=(2, 3, 4))
            come(K, 1, -d, ds=(-1, -2, -3))

        def third():
            come(K, 1, d, ds=(1, 2, 3))
            come(V, 1, -d, "zp", ds=(-1, -2, -3))
            arrived(V, 1, d)

            @pl.when(d < 3)
            def _():
                send(V, 1, d, "zm", ds=(1, 2))

            send(V, 1, d, "sib", ds=(1, 2, 3))
            sibling(0, -d, d)

        def fourth():
            @pl.when(d < 3)
            def _():
                arrived(V, 0, -d - 1)

            @pl.when(d == 1)
            def _():
                send(V, 0, -d - 1, "zp", ds=(-2,))

            @pl.when(d < 3)
            def _():
                send(V, 0, -d - 1, "sib", ds=(-2, -3))

            arrived(V, 0, d + 1)

            @pl.when(d < 3)
            def _():
                send(V, 0, d + 1, "zm", ds=(2, 3))

            send(V, 0, d + 1, "sib", ds=(2, 3, 4))

            @pl.when(d == 3)
            def _():
                sibling(1, -d, d)

        work(
            (first, 2 * d - 2, 0, None),
            (second, 2 * d - 2, 1, None),
            (third, 2 * d - 1, 0, None),
            (fourth, jnp.where(d == 3, NZ - 2, 2 * d - 1), jnp.where(d == 3, 0, 1), None),
        )
        return carry

    lax.fori_loop(1, 4, round_of, 0)
    come(K, 1, 4)
    come(V, 1, 4)
    sibling(0, 4)
    sibling(1, 4)

    results = []

    def result_copy(t, part, i):
        jp = t % 3
        ctx, base = (xb, (1 - xh) * 4) if t < 3 else (me, xh * 4)
        return pltpu.make_async_remote_copy(
            ost.at[t, pl.ds(pl.multiple_of(part * ROWS, ROWS), ROWS), :],
            out_ref.at[:, pl.ds(pl.multiple_of(h * FEAT + jp * TILE, TILE), TILE)],
            out_send.at[i], out_recv.at[h, jp],
            device_id=(ctx, base + part), device_id_type=MESH)

    def own_result(t):
        jp = t % 3
        return pltpu.make_async_copy(
            ost.at[t, pl.ds(pl.multiple_of(y * ROWS, ROWS), ROWS), :],
            out_ref.at[:, pl.ds(pl.multiple_of(h * FEAT + jp * TILE, TILE), TILE)],
            loc_sem.at[4 + jp])

    gates.wait()

    def done(t, total):
        slot = t // 3
        jp = t % 3
        scaled = total[:HD] * (1.0 / total[HD:HD + 1])
        for jj in range(2):
            j = 2 * jp + jj
            rows = scaled[:, jj * HD:(jj + 1) * HD].T
            rows = rows * gate_rows[slot][:, j * HD:(j + 1) * HD]
            rows = jnp.where(live[slot], rows, jnp.float32(0))
            ost[t, :, jj * HD:(jj + 1) * HD] = rows.astype(jnp.bfloat16)
        for r in range(4):
            part = lax.rem(y + r, 4)
            if slot == 1 and r == 0:
                own_result(t).start()
                continue
            result_copy(t, part, len(results)).start()
            results.append((t, part))

    work((None, NZ - 1, 0, done), *((None, NZ - 3 + i, 1, done if i == 2 else None) for i in range(3)))

    for jp in range(3):
        own_result(3 + jp).wait()
    for i, (t, part) in enumerate(results):
        result_copy(t, part, i).wait_send()
    for i, peer in enumerate(peers):
        for copy in (k_copy, v_copy, q_copy):
            copy(i, peer[3], peer[0]).wait_send()
    for half, column, d, link in sent:
        block_copy(half, me, link, column, d).wait_send()
    for ctx, head, _, _ in peers:
        for jp in range(3):
            pltpu.make_async_remote_copy(
                ost.at[0, pl.ds(0, ROWS), :],
                out_ref.at[:, pl.ds(pl.multiple_of(head * FEAT + jp * TILE, TILE), TILE)],
                out_send.at[0], out_recv.at[head, jp],
                device_id=(ctx, head), device_id_type=MESH).wait_recv()


def local(queries, keys, values, fold_map, noisy, noise_step, gate_table):
    hbm = pl.BlockSpec(memory_space=pl.ANY)
    smem = pl.BlockSpec(memory_space=pltpu.SMEM)
    width = 2 * SPAN * RATIO
    blocks = NZ * 4
    return pl.pallas_call(
        kernel,
        out_shape=jax.ShapeDtypeStruct(queries.shape, queries.dtype),
        in_specs=[hbm, hbm, hbm, smem, smem, smem, hbm],
        out_specs=hbm,
        scratch_shapes=[
            pltpu.VMEM((NH, ROWS, FEAT), jnp.bfloat16),
            pltpu.VMEM(keys.shape, jnp.bfloat16),
            pltpu.VMEM(values.shape, jnp.bfloat16),
            pltpu.VMEM((blocks, BLOCK, HD), jnp.bfloat16),
            pltpu.VMEM((BLOCK, HD), jnp.bfloat16),
            pltpu.VMEM((blocks, VROWS, BLOCK), jnp.bfloat16),
            pltpu.VMEM((2 * HD, width), jnp.bfloat16),
            pltpu.VMEM((8, width), jnp.float32),
            pltpu.VMEM((VROWS, width), jnp.float32),
            pltpu.VMEM(gate_table.shape, jnp.float32),
            pltpu.VMEM((TILES, SPAN, TILE), jnp.bfloat16),
            pltpu.SemaphoreType.DMA((3, NH)),
            pltpu.SemaphoreType.DMA((3, NH)),
            pltpu.SemaphoreType.DMA((8,)),
            pltpu.SemaphoreType.DMA((4, 2, 2 * NZ)),
            pltpu.SemaphoreType.DMA((2, blocks)),
            pltpu.SemaphoreType.DMA((24,)),
            pltpu.SemaphoreType.DMA((NH, 3)),
        ],
        compiler_params=pltpu.CompilerParams(
            collective_id=0, has_side_effects=True, vmem_limit_bytes=60 * 2**20
        ),
        cost_estimate=pl.CostEstimate(
            flops=2 * 2 * width * 8192 * HD, bytes_accessed=2**20, transcendentals=width * 8192
        ),
    )(queries, keys, values, fold_map, noisy, noise_step, gate_table)


def solution(mesh):
    placed = (
        P(("ctx", "head"), None),
        P(("ctx", "head"), None),
        P(("ctx", "head"), None),
        P(),
        P(),
        P(),
        P(None, "head"),
    )
    return jax.shard_map(
        local, mesh=mesh, in_specs=placed, out_specs=P(("ctx", "head"), None), check_vma=False
    )
```

```python
import functools
import math

import jax
import jax.numpy as jnp
from jax import lax
from jax.experimental import pallas as pl
from jax.experimental.pallas import tpu as pltpu
from jax.sharding import PartitionSpec as P

HEADS = 48
KVH = 8
HD = 128
SPAN = 128
NZ = 8
NH = 8
RATIO = HEADS // KVH
ROWS = 32
BLOCK = NH * ROWS
GROUP = 4 * BLOCK
FEAT = RATIO * HD
TILE = 256
TILES = 2 * SPAN * RATIO // TILE
VROWS = HD + 16
NEG = -1e30
MESH = pl.DeviceIdType.MESH
K, V = 0, 1


def kernel(
    q_ref, k_ref, v_ref, fold, noisy, noise_step, gate_ref, out_ref,
    q_in, k_loc, v_loc, k_buf, v_in, vt_buf, qt, m_s, acc, gate_v, ost,
    a2a_send, a2a_recv, loc_sem, kv_send, kv_recv, out_send, out_recv,
):
    me = lax.axis_index("ctx")
    h = lax.axis_index("head")
    z = lax.div(me, 4)
    x = lax.rem(lax.div(me, 2), 2)
    c = lax.rem(me, 2)
    xh = lax.div(h, 4)
    y = lax.rem(h, 4)

    def ctx_of(dz, x_, c_):
        return lax.rem(z + (dz + NZ), NZ) * 4 + x_ * 2 + c_

    zp, zm = ctx_of(1, x, c), ctx_of(-1, x, c)
    xb, sib = ctx_of(0, 1 - x, c), ctx_of(0, x, 1 - c)
    peers = [(me, xh * 4 + lax.rem(y + r, 4), 4 + lax.rem(y + r, 4), 4 + y) for r in (2, 1, 3)]
    peers += [(xb, (1 - xh) * 4 + lax.rem(y + r, 4), lax.rem(y + r, 4), y) for r in (2, 1, 3, 0)]
    mine = 4 + y

    stage_k = pltpu.make_async_copy(k_ref, k_loc, loc_sem.at[0])
    stage_v = pltpu.make_async_copy(v_ref, v_loc, loc_sem.at[1])
    own_q = pltpu.make_async_copy(
        q_ref.at[:, pl.ds(pl.multiple_of(h * FEAT, FEAT), FEAT)], q_in.at[mine], loc_sem.at[2])
    gates = pltpu.make_async_copy(gate_ref, gate_v, loc_sem.at[3])
    stage_k.start()
    stage_v.start()
    own_q.start()
    gates.start()

    barrier = pltpu.get_barrier_semaphore()
    for ctx, head, _, _ in peers:
        pl.semaphore_signal(barrier, inc=1, device_id=(ctx, head), device_id_type=MESH)
    for other in (zp, zm, xb, sib):
        pl.semaphore_signal(barrier, inc=1, device_id=(other, h), device_id_type=MESH)
    vt_buf[:, HD:, :] = jnp.ones((NZ * 4, VROWS - HD, BLOCK), jnp.bfloat16)
    m_s[...] = jnp.full_like(m_s, NEG)
    acc[...] = jnp.zeros_like(acc)
    stage_k.wait()
    stage_v.wait()
    pl.semaphore_wait(barrier, NH - 1 + 4)

    def k_copy(i, slot, block):
        ctx, head, _, _ = peers[i]
        return pltpu.make_async_remote_copy(
            k_loc.at[:, pl.ds(pl.multiple_of(head * HD, HD), HD)],
            k_buf.at[block, pl.ds(pl.multiple_of(slot * ROWS, ROWS), ROWS), :],
            a2a_send.at[0, i], a2a_recv.at[0, slot], device_id=(ctx, head), device_id_type=MESH)

    def v_copy(i, slot, block):
        ctx, head, _, _ = peers[i]
        return pltpu.make_async_remote_copy(
            v_loc.at[:, pl.ds(pl.multiple_of(head * HD, HD), HD)],
            v_in.at[pl.ds(pl.multiple_of(slot * ROWS, ROWS), ROWS), :],
            a2a_send.at[1, i], a2a_recv.at[1, slot], device_id=(ctx, head), device_id_type=MESH)

    def q_copy(i, slot, block):
        ctx, head, _, _ = peers[i]
        return pltpu.make_async_remote_copy(
            q_ref.at[:, pl.ds(pl.multiple_of(head * FEAT, FEAT), FEAT)], q_in.at[slot],
            a2a_send.at[2, i], a2a_recv.at[2, slot], device_id=(ctx, head), device_id_type=MESH)

    for copy in (k_copy, v_copy, q_copy):
        for i, peer in enumerate(peers):
            copy(i, peer[3], peer[0]).start()
    here = pl.ds(pl.multiple_of(h * HD, HD), HD)
    rows_here = pl.ds(pl.multiple_of(mine * ROWS, ROWS), ROWS)
    k_buf[me, rows_here, :] = k_loc[:, here]
    v_in[rows_here, :] = v_loc[:, here]

    sent = []
    targets = dict(zp=zp, zm=zm, xb=xb, sib=sib)
    links = list(targets)

    def block_of(column, d, core):
        return ctx_of(d, x if column == 0 else 1 - x, core)

    def block_copy(half, block, link, column, d):
        ref = k_buf.at[block] if half == K else vt_buf.at[block, pl.ds(0, HD), :]
        return pltpu.make_async_remote_copy(
            ref, ref, kv_send.at[links.index(link), half, column * NZ + lax.rem(d + NZ, NZ)],
            kv_recv.at[half, block], device_id=(targets[link], h), device_id_type=MESH)

    def send(half, column, d, *onto, ds=None):
        for link in onto:
            block_copy(half, block_of(column, d, c), link, column, d).start()
            for value in (d,) if ds is None else ds:
                sent.append((half, column, value, link))

    def arrived(half, column, d, core=c):
        block_copy(half, block_of(column, d, core), "sib", column, d).wait_recv()

    def come(half, column, d, *onto, ds=None):
        arrived(half, column, d)
        send(half, column, d, *onto, "sib", ds=ds)

    def sibling(column, *steps):
        for d in steps:
            for half in (K, V):
                arrived(half, column, d, 1 - c)

    for i, peer in enumerate(peers):
        k_copy(i, peer[2], me).wait_recv()
    send(K, 0, 0, *links)
    for i, peer in enumerate(peers):
        v_copy(i, peer[2], me).wait_recv()
    vt_buf[me, :HD, :] = v_in[...].astype(jnp.float32).T.astype(jnp.bfloat16)
    send(V, 0, 0, *links)

    come(K, 1, 0)
    come(K, 0, -1, "zp", "xb")
    come(K, 0, 1, "zm", "xb")
    come(V, 1, 0, "zp", "zm")
    come(V, 0, -1, "zp")
    come(V, 0, 1, "zm")

    own_q.wait()
    for i, peer in enumerate(peers):
        q_copy(i, peer[2], me).wait_recv()
    factor = math.log2(math.e) / math.sqrt(HD)
    for slot in range(2):
        for j in range(RATIO):
            part = q_in[slot * 4:slot * 4 + 4, :, j * HD:(j + 1) * HD].reshape(SPAN, HD)
            scaled = (part.astype(jnp.float32) * factor).T
            high = scaled.astype(jnp.bfloat16)
            low = (scaled - high.astype(jnp.float32)).astype(jnp.bfloat16)
            at = (slot * RATIO + j) * HD
            qt[0:HD, at:at + HD] = high
            qt[HD:2 * HD, at:at + HD] = low

    my_order = [fold[2 * xb + 1 - xh], fold[2 * me + xh]]
    gate_rows = [gate_v.at[pl.ds(noise_step[o], 1), :] for o in my_order]
    live = [noisy[o] == 1 for o in my_order]

    def group(i):
        away = lax.div(i + 1, 2)
        col_a = jnp.where(lax.rem(i, 2) == 1, x, 1 - x)
        col_b = jnp.where((i == 0) | (i == NZ - 1), 1 - col_a, col_a)
        pairs = []
        for zq, col in ((lax.rem(z + away, NZ), col_a), (lax.rem(z + NZ - away, NZ), col_b)):
            pairs.append((zq * 4 + col * 2, 2 - 4 * col))
        keys = jnp.concatenate([k_buf[pl.ds(b, 2)].reshape(2 * BLOCK, HD) for b, _ in pairs], axis=0)
        keys = jnp.concatenate([keys, keys], axis=1)
        values = jnp.concatenate([vt_buf[b + core] for b, _ in pairs for core in range(2)], axis=1)
        orders = []
        for b, flip in pairs:
            for core in range(2):
                orders.append(fold[2 * (b + core + flip) + 1 - xh])
                orders.append(fold[2 * (b + core) + xh])
        return keys, values, orders

    def work(*parts):
        half = TILES // 2
        units = [(p, t) for p in range(len(parts)) for t in range(half)]
        groups = {}

        def enter(p):
            before, number, slot, _ = parts[p]
            if before is not None:
                before()
            order = my_order[slot] if isinstance(slot, int) else jnp.where(slot == 0, my_order[0], my_order[1])
            keys, values, orders = group(number)
            groups[p] = keys, values, [jnp.where(o <= order, jnp.float32(0), jnp.float32(NEG)) for o in orders]

        def cols(p, t):
            return pl.ds(pl.multiple_of((parts[p][2] * half + t) * TILE, TILE), TILE)

        def score(p, t):
            if p not in groups:
                enter(p)
            return jnp.dot(groups[p][0], qt[:, cols(p, t)], preferred_element_type=jnp.float32)

        def soften(p, t, s):
            bias = groups[p][2]
            before = m_s[0:1, cols(p, t)]
            top = before
            for i, b in enumerate(bias):
                top = jnp.maximum(top, jnp.max(s[i * SPAN:(i + 1) * SPAN], axis=0, keepdims=True) + b)
            probs = [
                jnp.exp2(s[i * SPAN:(i + 1) * SPAN] - (top - 2 * b)).astype(jnp.bfloat16)
                for i, b in enumerate(bias)
            ]
            m_s[0:1, cols(p, t)] = top
            return jnp.concatenate(probs, axis=0), jnp.exp2(before - top)

        def add(p, t, probs, alpha):
            total = acc[:, cols(p, t)] * alpha + jnp.dot(groups[p][1], probs, preferred_element_type=jnp.float32)
            if parts[p][3] is None:
                acc[:, cols(p, t)] = total
            else:
                parts[p][3](parts[p][2] * half + t, total)

        s = score(*units[0])
        held = None
        for n, unit in enumerate(units):
            following = score(*units[n + 1]) if n + 1 < len(units) else None
            if held is not None:
                add(*units[n - 1], *held)
            held = soften(*unit, s)
            s = following
        add(*units[-1], *held)

    def round_of(d, carry):
        def first():
            @pl.when(d == 1)
            def _():
                sibling(0, 0)
                sibling(1, 0)

            @pl.when(d > 1)
            def _():
                sibling(1, 1 - d, d - 1)

        def second():
            @pl.when(d < 3)
            def _():
                come(K, 0, -d - 1, "zp", "xb", ds=(-2, -3))

            arrived(K, 0, d + 1)

            @pl.when(d == 1)
            def _():
                send(K, 0, d + 1, "zm", ds=(2,))

            send(K, 0, d + 1, "xb", "sib", ds=(2, 3, 4))
            come(K, 1, -d, ds=(-1, -2, -3))

        def third():
            come(K, 1, d, ds=(1, 2, 3))
            come(V, 1, -d, "zp", ds=(-1, -2, -3))
            arrived(V, 1, d)

            @pl.when(d < 3)
            def _():
                send(V, 1, d, "zm", ds=(1, 2))

            send(V, 1, d, "sib", ds=(1, 2, 3))
            sibling(0, -d, d)

        def fourth():
            @pl.when(d < 3)
            def _():
                arrived(V, 0, -d - 1)

            @pl.when(d == 1)
            def _():
                send(V, 0, -d - 1, "zp", ds=(-2,))

            @pl.when(d < 3)
            def _():
                send(V, 0, -d - 1, "sib", ds=(-2, -3))

            arrived(V, 0, d + 1)

            @pl.when(d < 3)
            def _():
                send(V, 0, d + 1, "zm", ds=(2, 3))

            send(V, 0, d + 1, "sib", ds=(2, 3, 4))

            @pl.when(d == 3)
            def _():
                sibling(1, -d, d)

        work(
            (first, 2 * d - 2, 0, None),
            (second, 2 * d - 2, 1, None),
            (third, 2 * d - 1, 0, None),
            (fourth, jnp.where(d == 3, NZ - 2, 2 * d - 1), jnp.where(d == 3, 0, 1), None),
        )
        return carry

    lax.fori_loop(1, 4, round_of, 0)

    def opposite():
        come(K, 1, 4)
        come(V, 1, 4)
        sibling(0, 4)
        sibling(1, 4)

    results = []

    def result_copy(t, part, i):
        jp = t % 3
        ctx, base = (xb, (1 - xh) * 4) if t < 3 else (me, xh * 4)
        return pltpu.make_async_remote_copy(
            ost.at[t, pl.ds(pl.multiple_of(part * ROWS, ROWS), ROWS), :],
            out_ref.at[:, pl.ds(pl.multiple_of(h * FEAT + jp * TILE, TILE), TILE)],
            out_send.at[i], out_recv.at[h, jp],
            device_id=(ctx, base + part), device_id_type=MESH)

    def own_result(t):
        jp = t % 3
        return pltpu.make_async_copy(
            ost.at[t, pl.ds(pl.multiple_of(y * ROWS, ROWS), ROWS), :],
            out_ref.at[:, pl.ds(pl.multiple_of(h * FEAT + jp * TILE, TILE), TILE)],
            loc_sem.at[4 + jp])

    gates.wait()

    def done(t, total):
        slot = t // 3
        jp = t % 3
        scaled = total[:HD] * (1.0 / total[HD:HD + 1])
        for jj in range(2):
            j = 2 * jp + jj
            rows = scaled[:, jj * HD:(jj + 1) * HD].T
            rows = rows * gate_rows[slot][:, j * HD:(j + 1) * HD]
            rows = jnp.where(live[slot], rows, jnp.float32(0))
            ost[t, :, jj * HD:(jj + 1) * HD] = rows.astype(jnp.bfloat16)
        for r in range(4):
            part = lax.rem(y + r, 4)
            if slot == 1 and r == 0:
                own_result(t).start()
                continue
            result_copy(t, part, len(results)).start()
            results.append((t, part))

    work(
        (None, NZ - 3, 1, None),
        (opposite, NZ - 1, 0, done),
        (None, NZ - 2, 1, None),
        (None, NZ - 1, 1, done),
    )

    for jp in range(3):
        own_result(3 + jp).wait()
    for i, (t, part) in enumerate(results):
        result_copy(t, part, i).wait_send()
    for i, peer in enumerate(peers):
        for copy in (k_copy, v_copy, q_copy):
            copy(i, peer[3], peer[0]).wait_send()
    for half, column, d, link in sent:
        block_copy(half, me, link, column, d).wait_send()
    for ctx, head, _, _ in peers:
        for jp in range(3):
            pltpu.make_async_remote_copy(
                ost.at[0, pl.ds(0, ROWS), :],
                out_ref.at[:, pl.ds(pl.multiple_of(head * FEAT + jp * TILE, TILE), TILE)],
                out_send.at[0], out_recv.at[head, jp],
                device_id=(ctx, head), device_id_type=MESH).wait_recv()


def local(queries, keys, values, fold_map, noisy, noise_step, gate_table):
    hbm = pl.BlockSpec(memory_space=pl.ANY)
    smem = pl.BlockSpec(memory_space=pltpu.SMEM)
    width = 2 * SPAN * RATIO
    blocks = NZ * 4
    return pl.pallas_call(
        kernel,
        out_shape=jax.ShapeDtypeStruct(queries.shape, queries.dtype),
        in_specs=[hbm, hbm, hbm, smem, smem, smem, hbm],
        out_specs=hbm,
        scratch_shapes=[
            pltpu.VMEM((NH, ROWS, FEAT), jnp.bfloat16),
            pltpu.VMEM(keys.shape, jnp.bfloat16),
            pltpu.VMEM(values.shape, jnp.bfloat16),
            pltpu.VMEM((blocks, BLOCK, HD), jnp.bfloat16),
            pltpu.VMEM((BLOCK, HD), jnp.bfloat16),
            pltpu.VMEM((blocks, VROWS, BLOCK), jnp.bfloat16),
            pltpu.VMEM((2 * HD, width), jnp.bfloat16),
            pltpu.VMEM((8, width), jnp.float32),
            pltpu.VMEM((VROWS, width), jnp.float32),
            pltpu.VMEM(gate_table.shape, jnp.float32),
            pltpu.VMEM((TILES, SPAN, TILE), jnp.bfloat16),
            pltpu.SemaphoreType.DMA((3, NH)),
            pltpu.SemaphoreType.DMA((3, NH)),
            pltpu.SemaphoreType.DMA((8,)),
            pltpu.SemaphoreType.DMA((4, 2, 2 * NZ)),
            pltpu.SemaphoreType.DMA((2, blocks)),
            pltpu.SemaphoreType.DMA((24,)),
            pltpu.SemaphoreType.DMA((NH, 3)),
        ],
        compiler_params=pltpu.CompilerParams(
            collective_id=0, has_side_effects=True, vmem_limit_bytes=60 * 2**20
        ),
        cost_estimate=pl.CostEstimate(
            flops=2 * 2 * width * 8192 * HD, bytes_accessed=2**20, transcendentals=width * 8192
        ),
    )(queries, keys, values, fold_map, noisy, noise_step, gate_table)


def solution(mesh):
    placed = (
        P(("ctx", "head"), None),
        P(("ctx", "head"), None),
        P(("ctx", "head"), None),
        P(),
        P(),
        P(),
        P(None, "head"),
    )
    return jax.shard_map(
        local, mesh=mesh, in_specs=placed, out_specs=P(("ctx", "head"), None), check_vma=False
    )
```

```python
import functools
import math

import jax
import jax.numpy as jnp
from jax import lax
from jax.experimental import pallas as pl
from jax.experimental.pallas import tpu as pltpu
from jax.sharding import PartitionSpec as P

HEADS = 48
KVH = 8
HD = 128
SPAN = 128
NZ = 8
NH = 8
RATIO = HEADS // KVH
ROWS = 32
BLOCK = NH * ROWS
GROUP = 4 * BLOCK
FEAT = RATIO * HD
TILE = 256
TILES = 2 * SPAN * RATIO // TILE
VROWS = HD + 16
NEG = -1e30
MESH = pl.DeviceIdType.MESH
K, V = 0, 1


def kernel(
    q_ref, k_ref, v_ref, fold, noisy, noise_step, gate_ref, out_ref, live_ref,
    q_in, k_loc, v_loc, k_buf, v_in, vt_buf, qt, m_s, acc, gate_v, ost,
    a2a_send, a2a_recv, loc_sem, kv_send, kv_recv, out_send, out_recv,
):
    me = lax.axis_index("ctx")
    h = lax.axis_index("head")
    z = lax.div(me, 4)
    x = lax.rem(lax.div(me, 2), 2)
    c = lax.rem(me, 2)
    xh = lax.div(h, 4)
    y = lax.rem(h, 4)

    def ctx_of(dz, x_, c_):
        return lax.rem(z + (dz + NZ), NZ) * 4 + x_ * 2 + c_

    zp, zm = ctx_of(1, x, c), ctx_of(-1, x, c)
    xb, sib = ctx_of(0, 1 - x, c), ctx_of(0, x, 1 - c)
    peers = [(me, xh * 4 + lax.rem(y + r, 4), 4 + lax.rem(y + r, 4), 4 + y) for r in (2, 1, 3)]
    peers += [(xb, (1 - xh) * 4 + lax.rem(y + r, 4), lax.rem(y + r, 4), y) for r in (2, 1, 3, 0)]
    mine = 4 + y

    stage_k = pltpu.make_async_copy(k_ref, k_loc, loc_sem.at[0])
    stage_v = pltpu.make_async_copy(v_ref, v_loc, loc_sem.at[1])
    own_q = pltpu.make_async_copy(
        q_ref.at[:, pl.ds(pl.multiple_of(h * FEAT, FEAT), FEAT)], q_in.at[mine], loc_sem.at[2])
    gates = pltpu.make_async_copy(gate_ref, gate_v, loc_sem.at[3])
    stage_k.start()
    stage_v.start()
    own_q.start()
    gates.start()

    barrier = pltpu.get_barrier_semaphore()
    for ctx, head, _, _ in peers:
        pl.semaphore_signal(barrier, inc=1, device_id=(ctx, head), device_id_type=MESH)
    for other in (zp, zm, xb, sib):
        pl.semaphore_signal(barrier, inc=1, device_id=(other, h), device_id_type=MESH)
    vt_buf[:, HD:, :] = jnp.ones((NZ * 4, VROWS - HD, BLOCK), jnp.bfloat16)
    m_s[...] = jnp.full_like(m_s, NEG)
    acc[...] = jnp.zeros_like(acc)
    stage_k.wait()
    stage_v.wait()
    pl.semaphore_wait(barrier, NH - 1 + 4)

    def k_copy(i, slot, block):
        ctx, head, _, _ = peers[i]
        return pltpu.make_async_remote_copy(
            k_loc.at[:, pl.ds(pl.multiple_of(head * HD, HD), HD)],
            k_buf.at[block, pl.ds(pl.multiple_of(slot * ROWS, ROWS), ROWS), :],
            a2a_send.at[0, i], a2a_recv.at[0, slot], device_id=(ctx, head), device_id_type=MESH)

    def v_copy(i, slot, block):
        ctx, head, _, _ = peers[i]
        return pltpu.make_async_remote_copy(
            v_loc.at[:, pl.ds(pl.multiple_of(head * HD, HD), HD)],
            v_in.at[pl.ds(pl.multiple_of(slot * ROWS, ROWS), ROWS), :],
            a2a_send.at[1, i], a2a_recv.at[1, slot], device_id=(ctx, head), device_id_type=MESH)

    def q_copy(i, slot, block):
        ctx, head, _, _ = peers[i]
        return pltpu.make_async_remote_copy(
            q_ref.at[:, pl.ds(pl.multiple_of(head * FEAT, FEAT), FEAT)], q_in.at[slot],
            a2a_send.at[2, i], a2a_recv.at[2, slot], device_id=(ctx, head), device_id_type=MESH)

    for copy in (k_copy, v_copy, q_copy):
        for i, peer in enumerate(peers):
            copy(i, peer[3], peer[0]).start()
    here = pl.ds(pl.multiple_of(h * HD, HD), HD)
    rows_here = pl.ds(pl.multiple_of(mine * ROWS, ROWS), ROWS)
    k_buf[me, rows_here, :] = k_loc[:, here]
    v_in[rows_here, :] = v_loc[:, here]

    sent = []
    targets = dict(zp=zp, zm=zm, xb=xb, sib=sib)
    links = list(targets)

    def block_of(column, d, core):
        return ctx_of(d, x if column == 0 else 1 - x, core)

    def block_copy(half, block, link, column, d):
        ref = k_buf.at[block] if half == K else vt_buf.at[block, pl.ds(0, HD), :]
        return pltpu.make_async_remote_copy(
            ref, ref, kv_send.at[links.index(link), half, column * NZ + lax.rem(d + NZ, NZ)],
            kv_recv.at[half, block], device_id=(targets[link], h), device_id_type=MESH)

    def send(half, column, d, *onto, ds=None):
        for link in onto:
            block_copy(half, block_of(column, d, c), link, column, d).start()
            for value in (d,) if ds is None else ds:
                sent.append((half, column, value, link))

    def arrived(half, column, d, core=c):
        block_copy(half, block_of(column, d, core), "sib", column, d).wait_recv()

    def come(half, column, d, *onto, ds=None):
        arrived(half, column, d)
        send(half, column, d, *onto, "sib", ds=ds)

    def sibling(column, *steps):
        for d in steps:
            for half in (K, V):
                arrived(half, column, d, 1 - c)

    for i, peer in enumerate(peers):
        k_copy(i, peer[2], me).wait_recv()
    send(K, 0, 0, *links)
    for i, peer in enumerate(peers):
        v_copy(i, peer[2], me).wait_recv()
    vt_buf[me, :HD, :] = v_in[...].astype(jnp.float32).T.astype(jnp.bfloat16)
    send(V, 0, 0, *links)

    come(K, 1, 0)
    come(K, 0, -1, "zp", "xb")
    come(K, 0, 1, "zm", "xb")
    come(V, 1, 0, "zp", "zm")
    come(V, 0, -1, "zp")
    come(V, 0, 1, "zm")

    own_q.wait()
    for i, peer in enumerate(peers):
        q_copy(i, peer[2], me).wait_recv()
    factor = math.log2(math.e) / math.sqrt(HD)
    for slot in range(2):
        for j in range(RATIO):
            part = q_in[slot * 4:slot * 4 + 4, :, j * HD:(j + 1) * HD].reshape(SPAN, HD)
            scaled = (part.astype(jnp.float32) * factor).T
            high = scaled.astype(jnp.bfloat16)
            low = (scaled - high.astype(jnp.float32)).astype(jnp.bfloat16)
            at = (slot * RATIO + j) * HD
            qt[0:HD, at:at + HD] = high
            qt[HD:2 * HD, at:at + HD] = low

    my_order = [fold[2 * xb + 1 - xh], fold[2 * me + xh]]
    gate_rows = [gate_v.at[pl.ds(noise_step[o], 1), :] for o in my_order]
    live_ref[...] = jnp.full(live_ref.shape, jnp.where(noisy[my_order[1]] == 1, jnp.float32(1), jnp.float32(0)))

    def group(i):
        away = lax.div(i + 1, 2)
        col_a = jnp.where(lax.rem(i, 2) == 1, x, 1 - x)
        col_b = jnp.where((i == 0) | (i == NZ - 1), 1 - col_a, col_a)
        pairs = []
        for zq, col in ((lax.rem(z + away, NZ), col_a), (lax.rem(z + NZ - away, NZ), col_b)):
            pairs.append((zq * 4 + col * 2, 2 - 4 * col))
        keys = jnp.concatenate([k_buf[pl.ds(b, 2)].reshape(2 * BLOCK, HD) for b, _ in pairs], axis=0)
        keys = jnp.concatenate([keys, keys], axis=1)
        values = jnp.concatenate([vt_buf[b + core] for b, _ in pairs for core in range(2)], axis=1)
        orders = []
        for b, flip in pairs:
            for core in range(2):
                orders.append(fold[2 * (b + core + flip) + 1 - xh])
                orders.append(fold[2 * (b + core) + xh])
        return keys, values, orders

    def work(*parts):
        half = TILES // 2
        units = [(p, t) for p in range(len(parts)) for t in range(half)]
        groups = {}

        def enter(p):
            before, number, slot, _ = parts[p]
            if before is not None:
                before()
            order = my_order[slot] if isinstance(slot, int) else jnp.where(slot == 0, my_order[0], my_order[1])
            keys, values, orders = group(number)
            groups[p] = keys, values, [jnp.where(o <= order, jnp.float32(0), jnp.float32(NEG)) for o in orders]

        def cols(p, t):
            return pl.ds(pl.multiple_of((parts[p][2] * half + t) * TILE, TILE), TILE)

        def score(p, t):
            if p not in groups:
                enter(p)
            return jnp.dot(groups[p][0], qt[:, cols(p, t)], preferred_element_type=jnp.float32)

        def soften(p, t, s):
            bias = groups[p][2]
            before = m_s[0:1, cols(p, t)]
            top = before
            for i, b in enumerate(bias):
                top = jnp.maximum(top, jnp.max(s[i * SPAN:(i + 1) * SPAN], axis=0, keepdims=True) + b)
            probs = [
                jnp.exp2(s[i * SPAN:(i + 1) * SPAN] - (top - 2 * b)).astype(jnp.bfloat16)
                for i, b in enumerate(bias)
            ]
            m_s[0:1, cols(p, t)] = top
            return jnp.concatenate(probs, axis=0), jnp.exp2(before - top)

        def add(p, t, probs, alpha):
            total = acc[:, cols(p, t)] * alpha + jnp.dot(groups[p][1], probs, preferred_element_type=jnp.float32)
            if parts[p][3] is None:
                acc[:, cols(p, t)] = total
            else:
                parts[p][3](parts[p][2] * half + t, total)

        s = score(*units[0])
        held = None
        for n, unit in enumerate(units):
            following = score(*units[n + 1]) if n + 1 < len(units) else None
            if held is not None:
                add(*units[n - 1], *held)
            held = soften(*unit, s)
            s = following
        add(*units[-1], *held)

    def round_of(d, carry):
        def first():
            @pl.when(d == 1)
            def _():
                sibling(0, 0)
                sibling(1, 0)

            @pl.when(d > 1)
            def _():
                sibling(1, 1 - d, d - 1)

        def second():
            @pl.when(d < 3)
            def _():
                come(K, 0, -d - 1, "zp", "xb", ds=(-2, -3))

            arrived(K, 0, d + 1)

            @pl.when(d == 1)
            def _():
                send(K, 0, d + 1, "zm", ds=(2,))

            send(K, 0, d + 1, "xb", "sib", ds=(2, 3, 4))
            come(K, 1, -d, ds=(-1, -2, -3))

        def third():
            come(K, 1, d, ds=(1, 2, 3))
            come(V, 1, -d, "zp", ds=(-1, -2, -3))
            arrived(V, 1, d)

            @pl.when(d < 3)
            def _():
                send(V, 1, d, "zm", ds=(1, 2))

            send(V, 1, d, "sib", ds=(1, 2, 3))
            sibling(0, -d, d)

        def fourth():
            @pl.when(d < 3)
            def _():
                arrived(V, 0, -d - 1)

            @pl.when(d == 1)
            def _():
                send(V, 0, -d - 1, "zp", ds=(-2,))

            @pl.when(d < 3)
            def _():
                send(V, 0, -d - 1, "sib", ds=(-2, -3))

            arrived(V, 0, d + 1)

            @pl.when(d < 3)
            def _():
                send(V, 0, d + 1, "zm", ds=(2, 3))

            send(V, 0, d + 1, "sib", ds=(2, 3, 4))

            @pl.when(d == 3)
            def _():
                sibling(1, -d, d)

        work(
            (first, 2 * d - 2, 0, None),
            (second, 2 * d - 2, 1, None),
            (third, 2 * d - 1, 0, None),
            (fourth, jnp.where(d == 3, NZ - 2, 2 * d - 1), jnp.where(d == 3, 0, 1), None),
        )
        return carry

    lax.fori_loop(1, 4, round_of, 0)

    def opposite():
        come(K, 1, 4)
        come(V, 1, 4)
        sibling(0, 4)
        sibling(1, 4)

    results = []

    def result_copy(t, part, i):
        jp = t % 3
        ctx, base = (xb, (1 - xh) * 4) if t < 3 else (me, xh * 4)
        return pltpu.make_async_remote_copy(
            ost.at[t, pl.ds(pl.multiple_of(part * ROWS, ROWS), ROWS), :],
            out_ref.at[:, pl.ds(pl.multiple_of(h * FEAT + jp * TILE, TILE), TILE)],
            out_send.at[i], out_recv.at[h, jp],
            device_id=(ctx, base + part), device_id_type=MESH)

    def own_result(t):
        jp = t % 3
        return pltpu.make_async_copy(
            ost.at[t, pl.ds(pl.multiple_of(y * ROWS, ROWS), ROWS), :],
            out_ref.at[:, pl.ds(pl.multiple_of(h * FEAT + jp * TILE, TILE), TILE)],
            loc_sem.at[4 + jp])

    gates.wait()

    def done(t, total):
        slot = t // 3
        jp = t % 3
        scaled = total[:HD] * (1.0 / total[HD:HD + 1])
        for jj in range(2):
            j = 2 * jp + jj
            rows = scaled[:, jj * HD:(jj + 1) * HD].T
            rows = rows * gate_rows[slot][:, j * HD:(j + 1) * HD]
            ost[t, :, jj * HD:(jj + 1) * HD] = rows.astype(jnp.bfloat16)
        for r in range(4):
            part = lax.rem(y + r, 4)
            if slot == 1 and r == 0:
                own_result(t).start()
                continue
            result_copy(t, part, len(results)).start()
            results.append((t, part))

    work(
        (None, NZ - 3, 1, None),
        (opposite, NZ - 1, 0, done),
        (None, NZ - 2, 1, None),
        (None, NZ - 1, 1, done),
    )

    for jp in range(3):
        own_result(3 + jp).wait()
    for i, (t, part) in enumerate(results):
        result_copy(t, part, i).wait_send()
    for i, peer in enumerate(peers):
        for copy in (k_copy, v_copy, q_copy):
            copy(i, peer[3], peer[0]).wait_send()
    for half, column, d, link in sent:
        block_copy(half, me, link, column, d).wait_send()
    for ctx, head, _, _ in peers:
        for jp in range(3):
            pltpu.make_async_remote_copy(
                ost.at[0, pl.ds(0, ROWS), :],
                out_ref.at[:, pl.ds(pl.multiple_of(head * FEAT + jp * TILE, TILE), TILE)],
                out_send.at[0], out_recv.at[head, jp],
                device_id=(ctx, head), device_id_type=MESH).wait_recv()


def local(queries, keys, values, fold_map, noisy, noise_step, gate_table):
    hbm = pl.BlockSpec(memory_space=pl.ANY)
    smem = pl.BlockSpec(memory_space=pltpu.SMEM)
    width = 2 * SPAN * RATIO
    blocks = NZ * 4
    gated, live = pl.pallas_call(
        kernel,
        out_shape=(
            jax.ShapeDtypeStruct(queries.shape, queries.dtype),
            jax.ShapeDtypeStruct((8, queries.shape[1]), jnp.float32),
        ),
        in_specs=[hbm, hbm, hbm, smem, smem, smem, hbm],
        out_specs=(hbm, pl.BlockSpec(memory_space=pltpu.VMEM)),
        scratch_shapes=[
            pltpu.VMEM((NH, ROWS, FEAT), jnp.bfloat16),
            pltpu.VMEM(keys.shape, jnp.bfloat16),
            pltpu.VMEM(values.shape, jnp.bfloat16),
            pltpu.VMEM((blocks, BLOCK, HD), jnp.bfloat16),
            pltpu.VMEM((BLOCK, HD), jnp.bfloat16),
            pltpu.VMEM((blocks, VROWS, BLOCK), jnp.bfloat16),
            pltpu.VMEM((2 * HD, width), jnp.bfloat16),
            pltpu.VMEM((8, width), jnp.float32),
            pltpu.VMEM((VROWS, width), jnp.float32),
            pltpu.VMEM(gate_table.shape, jnp.float32),
            pltpu.VMEM((TILES, SPAN, TILE), jnp.bfloat16),
            pltpu.SemaphoreType.DMA((3, NH)),
            pltpu.SemaphoreType.DMA((3, NH)),
            pltpu.SemaphoreType.DMA((8,)),
            pltpu.SemaphoreType.DMA((4, 2, 2 * NZ)),
            pltpu.SemaphoreType.DMA((2, blocks)),
            pltpu.SemaphoreType.DMA((24,)),
            pltpu.SemaphoreType.DMA((NH, 3)),
        ],
        compiler_params=pltpu.CompilerParams(
            collective_id=0, has_side_effects=True, vmem_limit_bytes=60 * 2**20
        ),
        cost_estimate=pl.CostEstimate(
            flops=2 * 2 * width * 8192 * HD, bytes_accessed=2**20, transcendentals=width * 8192
        ),
    )(queries, keys, values, fold_map, noisy, noise_step, gate_table)
    return jnp.where(live[:1] > 0, gated, jnp.zeros_like(gated))


def solution(mesh):
    placed = (
        P(("ctx", "head"), None),
        P(("ctx", "head"), None),
        P(("ctx", "head"), None),
        P(),
        P(),
        P(),
        P(None, "head"),
    )
    return jax.shard_map(
        local, mesh=mesh, in_specs=placed, out_specs=P(("ctx", "head"), None), check_vma=False
    )
```
